128 devices in a mesh: fsdp: 64 (over y, x_hi, z, core), sp: 2 (over x_lo).
Axes of the slice: x: 4 (x_hi: 2, x_lo: 2; x = x_hi * 2 + x_lo), y: 4, z: 4, core: 2. Of those that a mesh axis runs over, the one named last changes fastest.
Arguments:
- inputs: bfloat16 [16384, 768], P(('fsdp', 'sp')), may hold values from -6 to 6
- cotangent: bfloat16 [16384, 768], P(('fsdp', 'sp')), may hold values from -6 to 6
- routes: int32 [16384, 1], P(('fsdp', 'sp')), may hold values from 0 to 15; in each aligned block of 128 rows (0 to 127, 128 to 255, ...) at most 10 rows name the same one
- drop_mask: int32 [16384], P(('fsdp', 'sp')), may hold values 0 or 1
- buckets: int32 [511], replicated, may hold values from 0 to 31
- qkv_weight: bfloat16 [768, 2304], P(('fsdp', 'sp')), may hold values from -0.078125 to 0.078125
- out_weight: bfloat16 [768, 768], P(('fsdp', 'sp')), may hold values from -3.5 to 3.5
- router_weight: bfloat16 [768, 16], P(('fsdp', 'sp')), may hold values from -0.15625 to 0.15625
- attn_gain: bfloat16 [768], P(('fsdp', 'sp')), may hold values from 0.5 to 1.5
- ffn_gain: bfloat16 [768], P(('fsdp', 'sp')), may hold values from 0.5 to 1.5
- bias_table: bfloat16 [384], P(('fsdp', 'sp')), may hold values from -4 to 4
- expert_in: bfloat16 [768, 49152], P(None, ('fsdp', 'sp')), may hold values from -0.21875 to 0.21875
- expert_out: bfloat16 [49152, 768], P(('fsdp', 'sp')), may hold values from -1.75 to 1.75
Outputs:
- result: bfloat16 [16384, 768], P(('fsdp', 'sp'))
- grad_input: bfloat16 [16384, 768], P(('fsdp', 'sp'))
- grad_qkv: float32 [768, 2304], P(('fsdp', 'sp'))
- grad_out_weight: float32 [768, 768], P(('fsdp', 'sp'))
- grad_router: float32 [768, 16], P(('fsdp', 'sp'))
- grad_attn_gain: float32 [768], P(('fsdp', 'sp'))
- grad_ffn_gain: float32 [768], P(('fsdp', 'sp'))
- grad_bias: float32 [384], P(('fsdp', 'sp'))
- grad_expert_in: float32 [768, 49152], P(None, ('fsdp', 'sp'))
- grad_expert_out: float32 [49152, 768], P(('fsdp', 'sp'))
The draws below stay inside these ranges and needn't reach their ends.
Inputs may be any that keep to these rules, and one draw needn't show every extreme that they name: `routes`: among the 128 tokens of one device no expert is named more than 10 times, a bound that some block reaches.
All inputs are finite; a program needn't handle non-finite values. No bound on the sum of `drop_mask` on one device may be relied on, other than what follows from the above.
Results may differ from the reference program's by a relative error of at most 0.03.
Values may be sent and summed in bfloat16 or wider, within the bound.
A program may use at most 128 MiB of HBM per device.

```python
import functools
import math
import jax
import jax.numpy as jnp
import numpy as np
from jax import lax

D = 768
HEADS = 12
HEAD_DIM = 64
FF = 3072
EXPERTS = 16
BUCKETS = 32
TOK_DEV = 128
LENGTH = 256
TOKENS = 16384
CAP = 10
REPL = 8
FF_DEV = 384
DEVICES = 128


def set_ends(values, stream_key, smallest, top_value):
    spot = [jax.random.randint(jax.random.fold_in(stream_key, axis), (), 0, length) for axis, length in enumerate(values.shape)]
    main_axis = values.shape.index(max(values.shape))
    beside = spot[:main_axis] + [(spot[main_axis] + 1) % values.shape[main_axis]] + spot[main_axis + 1:]
    return values.at[tuple(spot)].set(smallest).at[tuple(beside)].set(top_value)


def levels(own_key, shape, pieces, low, largest):
    level = 1.0
    for dim, parts in pieces:
        heights = jax.random.uniform(jax.random.fold_in(jax.random.fold_in(own_key, 6), dim), (parts,), jnp.float32, low / len(pieces), largest / len(pieces))
        level = level * jnp.repeat(jnp.exp(heights), shape[dim] // parts).reshape((-1,) + (1,) * (len(shape) - 1 - dim))
    return level


def deal_out(stream_key, own, number, rows, amount, top, reach, skew):
    sequence = jax.random.permutation(stream_key, amount)
    heavy_load, ordinary = portions_of(amount, rows * top, reach, skew, True), portions_of(amount, rows * top, reach, skew, False)
    places = jnp.arange(amount)

    def named(tallies, turn):
        used = int((tallies > 0).sum())
        fixed = max(1, used // 4)
        passed = fixed + (places - fixed + turn * (used - fixed)) % max(1, amount - fixed)
        return jnp.zeros((amount,), jnp.int32).at[sequence[jnp.where(places < fixed, places, passed)]].set(jnp.asarray(tallies, jnp.int32))

    tallies = jnp.where(number % 4 == 0, named(heavy_load, number // 4), named(ordinary, number - number // 4 - 1))
    mixed = jax.random.permutation(jax.random.fold_in(own, 3), amount)
    source_of, taker = mixed[0:amount // 2 * 2:2], mixed[1:amount // 2 * 2:2]
    margin = jnp.minimum(tallies[source_of] - 1, reach - tallies[taker]) // 2
    margin = jnp.where((source_of == sequence[0]) | (taker == sequence[0]) | (tallies[taker] == 0), 0, jnp.maximum(margin, 0))
    passed = jax.random.randint(jax.random.fold_in(own, 4), (amount // 2,), 0, 1 << 20) % (margin + 1)
    tallies = tallies.at[source_of].add(-passed).at[taker].add(passed)
    members = jnp.searchsorted(jnp.cumsum(tallies), jnp.arange(rows * top), side="right").astype(jnp.int32)
    table = members.reshape(top, rows).T
    table = table[jax.random.permutation(jax.random.fold_in(own, 1), rows)]
    turn = jax.random.randint(jax.random.fold_in(own, 2), (rows, 1), 0, top)
    return jnp.take_along_axis(table, (jnp.arange(top)[None, :] + turn) % top, axis=1)


def portions_of(count, total, limit, lean, full):
    loads = [(1 << 20) // math.isqrt(grade ** lean) + 1 for grade in range(1, count + 1)]
    largest = limit if full else min(limit, max(-(-total // count), total * loads[0] // sum(loads)))
    least = 1 if total - largest >= count - 1 else 0
    holding, spare = [largest] + [least] * (count - 1), total - largest - least * (count - 1)
    while spare > 0:
        movable = [i for i in range(1, count) if holding[i] < largest] or [i for i in range(1, count) if holding[i] < limit]
        whole, remaining = sum([loads[i] for i in movable]), spare
        for i in movable:
            extra = min(limit - holding[i], max(1, remaining * loads[i] // whole), spare)
            holding[i] = holding[i] + extra
            spare = spare - extra
    return np.array(holding)


def normal_values(stream_key, extent, spread, most, pieces=(), kind=jnp.bfloat16):
    loudness = levels(stream_key, extent, pieces, -0.22, 0.18) if pieces else 1.0
    entries = jax.random.normal(stream_key, extent, jnp.float32) * spread * loudness
    return jnp.minimum(jnp.maximum(entries, -most), most).astype(kind)


def setup_inputs(seed: int = 0) -> dict:
    splits = jax.random.split(jax.random.key(seed), 14)
    inputs = normal_values(splits[0], (TOKENS, D), 1.0, 6.0, ((0, 128),))
    cotangent = normal_values(splits[1], (TOKENS, D), 1.0, 6.0, ((0, 128),))
    routes_keys = jax.random.split(jax.random.fold_in(splits[2], 1), TOKENS // TOK_DEV)
    routes_turns = jax.random.permutation(jax.random.fold_in(splits[2], 3), TOKENS // TOK_DEV)
    routes = jax.vmap(lambda own, number: deal_out(jax.random.fold_in(splits[2], 2), own, number, TOK_DEV, EXPERTS, 1, CAP, 2))(routes_keys, routes_turns).reshape((TOKENS, 1))
    drop_mask = set_ends((jax.random.randint(splits[3], (TOKENS,), 0, 8) < 7).astype(jnp.int32), jax.random.fold_in(splits[3], 1), 0, 1)
    buckets = set_ends(jax.random.randint(splits[4], (2 * LENGTH - 1,), 0, BUCKETS), jax.random.fold_in(splits[4], 1), 0, BUCKETS - 1).astype(jnp.int32)
    qkv_weight = normal_values(splits[5], (D, 3 * D), (8 * D) ** -0.5, 0.078125, ((0, 128),))
    out_weight = normal_values(splits[6], (D, D), (max(D // 256, 1)) ** -0.5, 3.5, ((0, 128),))
    router_weight = normal_values(splits[7], (D, EXPERTS), (2 * D) ** -0.5, 0.15625, ((0, 128),))
    attn_gain = jnp.clip(1.0 + 0.1 * jax.random.normal(splits[8], (D,), jnp.float32), 0.5, 1.5).astype(jnp.bfloat16)
    ffn_gain = jnp.clip(1.0 + 0.1 * jax.random.normal(splits[9], (D,), jnp.float32), 0.5, 1.5).astype(jnp.bfloat16)
    bias_table = normal_values(splits[10], (BUCKETS * HEADS,), 1.0, 4.0, ((0, 128),))
    expert_in = normal_values(splits[11], (D, EXPERTS * FF), D ** -0.5, 0.21875, ((1, 128),))
    expert_out = normal_values(splits[12], (EXPERTS * FF, D), (max(FF // 256, 1)) ** -0.5, 1.75, ((0, 128),))
    return dict(inputs=inputs, cotangent=cotangent, routes=routes, drop_mask=drop_mask, buckets=buckets, qkv_weight=qkv_weight, out_weight=out_weight, router_weight=router_weight, attn_gain=attn_gain, ffn_gain=ffn_gain, bias_table=bias_table, expert_in=expert_in, expert_out=expert_out)


EPSILON = 1e-06
HIGHEST = lax.Precision.HIGHEST

@jax.custom_vjp
def low(v):
    return lax.optimization_barrier(v.astype(jnp.bfloat16)).astype(jnp.float32)

@jax.custom_vjp
def low_back(v):
    return v

def low_keep(v):
    return (low(v), None)

def low_pass(kept, grad):
    return (grad,)

def back_keep(v):
    return (v, None)

def back_low(kept, grad):
    return (low(grad),)
low.defvjp(low_keep, low_pass)
low_back.defvjp(back_keep, back_low)

def rms_norm(values, gain):
    scale = lax.rsqrt(lax.optimization_barrier(jnp.mean(values * values, axis=-1, keepdims=True)) + EPSILON)
    return values * scale * gain

def one_sequence(stacked, bias_full):
    queries = stacked[:, 0]
    keys_all = stacked[:, 1]
    values_all = stacked[:, 2]
    scores = low_back(jnp.einsum('qhd,khd->hqk', queries, keys_all, precision=HIGHEST) + bias_full)
    weights = low(jax.nn.softmax(scores, axis=-1))
    mixed = jnp.einsum('hqk,khd->qhd', weights, values_all, precision=HIGHEST)
    return low_back(low(mixed)).reshape(LENGTH, D)

def one_expert(item):
    rows_in, weight_a, weight_b = item
    summed = jnp.zeros_like(rows_in)
    for portion in range(REPL):
        first = portion * FF_DEV
        pre_act = low_back(jnp.dot(low_back(rows_in), weight_a[:, first:first + FF_DEV], precision=HIGHEST))
        activity = low(jax.nn.gelu(pre_act))
        summed = summed + low(jnp.dot(activity, weight_b[first:first + FF_DEV], precision=HIGHEST))
    return low_back(summed)

def forward(features, qkv_full, out_full, router_full, gain_one, gain_two, table_flat, expert_a, expert_b, routes, drop_mask, buckets):
    normed = low(rms_norm(features, gain_one))
    projected = low_back(low(jnp.dot(normed, qkv_full, precision=HIGHEST)))
    stacked = projected.reshape(TOKENS // LENGTH, LENGTH, 3, HEADS, HEAD_DIM)
    offset_bias = table_flat.reshape(BUCKETS, HEADS)[buckets]
    relative = jnp.arange(LENGTH, dtype=jnp.int32)[None, :] - jnp.arange(LENGTH, dtype=jnp.int32)[:, None] + LENGTH - 1
    bias_full = jnp.transpose(offset_bias[relative], (2, 0, 1))
    mixed = lax.map(jax.checkpoint(functools.partial(one_sequence, bias_full=bias_full)), stacked).reshape(TOKENS, D)
    after_attn = features + low_back(jnp.dot(mixed, out_full, precision=HIGHEST))
    normed_two = low(rms_norm(after_attn, gain_two))
    logits = low_back(jnp.dot(normed_two, router_full, precision=HIGHEST))
    router_probs = jax.nn.softmax(logits, axis=-1)
    chosen = routes[:, 0]
    expert_hot = chosen[:, None] == jnp.arange(EXPERTS, dtype=jnp.int32)[None, :]
    gates = lax.optimization_barrier(jnp.sum(jnp.where(expert_hot, router_probs, 0.0), axis=-1))
    kept = drop_mask.astype(features.dtype)
    running = jnp.cumsum(expert_hot.astype(jnp.int32).reshape(DEVICES, TOK_DEV, EXPERTS), axis=1).reshape(TOKENS, EXPERTS)
    slot_index = lax.optimization_barrier(jnp.sum(jnp.where(expert_hot, running, 0), axis=-1)) - 1
    source = jnp.arange(TOKENS, dtype=jnp.int32) // TOK_DEV
    flat_slot = ((source * EXPERTS + chosen) * CAP + slot_index).astype(jnp.int32)
    buffer = jnp.zeros((DEVICES * EXPERTS * CAP, D), features.dtype).at[flat_slot].add(normed_two * kept[:, None])
    buffer = buffer.reshape(DEVICES, EXPERTS, CAP, D).transpose(1, 0, 2, 3).reshape(EXPERTS, DEVICES * CAP, D)
    weight_in = expert_a.reshape(D, EXPERTS, FF).transpose(1, 0, 2)
    weight_out = expert_b.reshape(EXPERTS, FF, D)
    slot_out = lax.map(jax.checkpoint(one_expert), (buffer, weight_in, weight_out))
    slot_out = slot_out.reshape(EXPERTS, DEVICES, CAP, D).transpose(1, 0, 2, 3).reshape(DEVICES * EXPERTS * CAP, D)
    expert_tok = slot_out[flat_slot]
    return after_attn + (kept * gates)[:, None] * expert_tok

def reference(inputs, cotangent, routes, drop_mask, buckets, qkv_weight, out_weight, router_weight, attn_gain, ffn_gain, bias_table, expert_in, expert_out):
    floats = [arr.astype(jnp.float32) for arr in (inputs, qkv_weight, out_weight, router_weight, attn_gain, ffn_gain, bias_table, expert_in, expert_out)]

    def closed(*params):
        return forward(*params, routes, drop_mask, buckets)
    result, puller = jax.vjp(closed, *floats)
    grads = puller(cotangent.astype(jnp.float32))
    return (result.astype(jnp.bfloat16), grads[0].astype(jnp.bfloat16), grads[1], grads[2], grads[3], grads[4], grads[5], grads[6], grads[7], grads[8])
```

```python
import functools

import jax
import jax.numpy as jnp
import numpy as np
from jax import lax
from jax.experimental import pallas as pl
from jax.experimental.pallas import tpu as pltpu
from jax.sharding import PartitionSpec as P

HEADS = 12
HEAD_DIM = 64
EXPERTS = 16
BUCKETS = 32
CAP = 10
EPSILON = 1e-06
MESH = pl.DeviceIdType.MESH
BF = jnp.bfloat16
F32 = jnp.float32
ANY = pl.BlockSpec(memory_space=pl.ANY)
SLOT = 24
GELU_C = 0.7978845608028654
GELU_A = 0.044715


def flat_id():
    return lax.axis_index("fsdp") * 2 + lax.axis_index("sp")


def coords(flat):
    return (lax.div(flat, 2), lax.rem(flat, 2))


QUAD = (4, lambda f: lax.rem(f, 4), lambda f, k: f - lax.rem(f, 4) + k)
SAME_M = (32, lambda f: lax.div(f, 4), lambda f, k: 4 * k + lax.rem(f, 4))
SAME_R = (16, lambda f: lax.div(f, 8), lambda f, k: 8 * k + lax.rem(f, 8))
PLANE = (
    4,
    lambda f: lax.div(lax.rem(f, 8), 4) * 2 + lax.rem(f, 2),
    lambda f, k: lax.div(f, 8) * 8
    + lax.div(k, 2) * 4
    + lax.rem(lax.div(f, 2), 2) * 2
    + lax.rem(k, 2),
)
MATE = (
    2,
    lambda f: lax.rem(lax.div(f, 2), 2),
    lambda f, k: f - lax.rem(lax.div(f, 2), 2) * 2 + 2 * k,
)


def for_range(low, high, fn):
    if high - low <= 4:
        for j in range(low, high):
            fn(j)
    else:

        def step(j, carry):
            fn(j)
            return carry

        lax.fori_loop(low, high, step, 0)


def greet(f, group):
    size, pos, peer = group
    me = pos(f)
    barrier = pltpu.get_barrier_semaphore()

    def hello(j):
        pl.semaphore_signal(
            barrier,
            inc=1,
            device_id=coords(peer(f, lax.rem(me + j, size))),
            device_id_type=MESH,
        )

    for_range(1, size, hello)
    pl.semaphore_wait(barrier, size - 1)


def exchange_kernel(group, kinds, *refs):
    count = len(kinds)
    ins, outs = refs[:count], refs[count : 2 * count]
    send, recv, own = refs[2 * count :]
    size, pos, peer = group
    f = flat_id()
    me = pos(f)
    greet(f, group)

    def copy(a, j):
        p = lax.rem(me + j, size)
        return pltpu.make_async_remote_copy(
            src_ref=ins[a] if kinds[a] else ins[a].at[p],
            dst_ref=outs[a].at[me],
            send_sem=send.at[a, j],
            recv_sem=recv.at[a, j],
            device_id=coords(peer(f, p)),
            device_id_type=MESH,
        )

    def local(a):
        return pltpu.make_async_copy(
            ins[a] if kinds[a] else ins[a].at[me], outs[a].at[me], own.at[a]
        )

    def start(j):
        for a in range(count):
            copy(a, j).start()

    def wait(j):
        for a in range(count):
            copy(a, j).wait()

    for_range(1, size, start)
    for a in range(count):
        local(a).start()
    for a in range(count):
        local(a).wait()
    for_range(1, size, wait)


def exchange(cid, group, *items):
    size = group[0]
    arrays = [array for array, gather in items]
    kinds = tuple(gather for array, gather in items)
    out = [
        jax.ShapeDtypeStruct((size,) + (a.shape if k else a.shape[1:]), a.dtype)
        for a, k in zip(arrays, kinds)
    ]
    moved = sum(a.size * a.dtype.itemsize * (size if k else 1) for a, k in zip(arrays, kinds))
    return pl.pallas_call(
        functools.partial(exchange_kernel, group, kinds),
        out_shape=out,
        in_specs=[ANY] * len(arrays),
        out_specs=[ANY] * len(arrays),
        scratch_shapes=[
            pltpu.SemaphoreType.DMA((len(arrays), size)),
            pltpu.SemaphoreType.DMA((len(arrays), size)),
            pltpu.SemaphoreType.DMA((len(arrays),)),
        ],
        compiler_params=pltpu.CompilerParams(collective_id=cid, has_side_effects=True),
        cost_estimate=pl.CostEstimate(flops=0, bytes_accessed=2 * moved, transcendentals=0),
    )(*arrays)


def weights_kernel(a_in, b_in, a_out, b_out, send_a, recv_a, send_b, recv_b, own):
    f = flat_id()
    m, g = lax.rem(f, 4), lax.div(f, 4)
    plane, place = lax.div(g, 8), lax.rem(g, 8)
    greet(f, SAME_M)

    def copy_a(j):
        return pltpu.make_async_remote_copy(
            src_ref=a_in,
            dst_ref=a_out.at[g],
            send_sem=send_a.at[j],
            recv_sem=recv_a.at[j],
            device_id=coords(4 * lax.rem(g + j, 32) + m),
            device_id_type=MESH,
        )

    def copy_b(j, q):
        return pltpu.make_async_remote_copy(
            src_ref=b_in,
            dst_ref=b_out.at[q],
            send_sem=send_b.at[j],
            recv_sem=recv_b.at[q],
            device_id=coords(4 * lax.rem(g + j, 32) + m),
            device_id_type=MESH,
        )

    for_range(1, 32, lambda j: copy_a(j).start())
    mine_a = pltpu.make_async_copy(a_in, a_out.at[g], own.at[0])
    mine_a.start()

    @pl.when(plane == m)
    def _():
        for_range(1, 32, lambda j: copy_b(j, place).start())
        mine_b = pltpu.make_async_copy(b_in, b_out.at[place], own.at[1])
        mine_b.start()
        mine_b.wait()

    mine_a.wait()
    for_range(1, 32, lambda j: copy_a(j).wait())

    def take(q):
        @pl.when(8 * m + q != g)
        def _():
            copy_b(1, q).wait_recv()

    for_range(0, 8, take)

    @pl.when(plane == m)
    def _():
        for_range(1, 32, lambda j: copy_b(j, place).wait_send())


def gather_weights(cid, a, b):
    return pl.pallas_call(
        weights_kernel,
        out_shape=[
            jax.ShapeDtypeStruct((32,) + a.shape, a.dtype),
            jax.ShapeDtypeStruct((8,) + b.shape, b.dtype),
        ],
        in_specs=[ANY] * 2,
        out_specs=[ANY] * 2,
        scratch_shapes=[
            pltpu.SemaphoreType.DMA((32,)),
            pltpu.SemaphoreType.DMA((32,)),
            pltpu.SemaphoreType.DMA((32,)),
            pltpu.SemaphoreType.DMA((8,)),
            pltpu.SemaphoreType.DMA((2,)),
        ],
        compiler_params=pltpu.CompilerParams(collective_id=cid, has_side_effects=True),
    )(a, b)


def grads_kernel(a_in, b_in, a_out, b_out, send_a, recv_a, send_b, recv_b, own):
    f = flat_id()
    m, g = lax.rem(f, 4), lax.div(f, 4)
    plane, place = lax.div(g, 8), lax.rem(g, 8)
    greet(f, SAME_M)

    def copy_a(j):
        p = lax.rem(g + j, 32)
        return pltpu.make_async_remote_copy(
            src_ref=a_in.at[p],
            dst_ref=a_out.at[g],
            send_sem=send_a.at[j],
            recv_sem=recv_a.at[j],
            device_id=coords(4 * p + m),
            device_id_type=MESH,
        )

    def copy_b(q):
        p = 8 * m + q
        return pltpu.make_async_remote_copy(
            src_ref=b_in.at[q],
            dst_ref=b_out.at[g],
            send_sem=send_b.at[q],
            recv_sem=recv_b.at[lax.rem(p - g + 32, 32)],
            device_id=coords(4 * p + m),
            device_id_type=MESH,
        )

    def away(q, fn):
        @pl.when(8 * m + q != g)
        def _():
            fn(q)

    for_range(0, 8, lambda q: away(q, lambda k: copy_b(k).start()))
    for_range(1, 32, lambda j: copy_a(j).start())
    mine_a = pltpu.make_async_copy(a_in.at[g], a_out.at[g], own.at[0])
    mine_a.start()

    @pl.when(plane == m)
    def _():
        mine_b = pltpu.make_async_copy(b_in.at[place], b_out.at[g], own.at[1])
        mine_b.start()
        mine_b.wait()

    mine_a.wait()
    for_range(1, 32, lambda j: copy_a(j).wait())
    for_range(0, 8, lambda q: away(q, lambda k: copy_b(k).wait_send()))

    @pl.when(plane == m)
    def _():
        def take(j):
            sender = lax.rem(g - j + 32, 32)
            pltpu.make_async_remote_copy(
                src_ref=b_in.at[0],
                dst_ref=b_out.at[sender],
                send_sem=send_b.at[0],
                recv_sem=recv_b.at[j],
                device_id=coords(4 * sender + m),
                device_id_type=MESH,
            ).wait_recv()

        for_range(1, 32, take)


def scatter_grads(cid, a, b):
    return pl.pallas_call(
        grads_kernel,
        out_shape=[
            jax.ShapeDtypeStruct(a.shape, a.dtype),
            jax.ShapeDtypeStruct((32,) + b.shape[1:], b.dtype),
        ],
        in_specs=[ANY] * 2,
        out_specs=[ANY] * 2,
        scratch_shapes=[
            pltpu.SemaphoreType.DMA((32,)),
            pltpu.SemaphoreType.DMA((32,)),
            pltpu.SemaphoreType.DMA((8,)),
            pltpu.SemaphoreType.DMA((32,)),
            pltpu.SemaphoreType.DMA((2,)),
        ],
        compiler_params=pltpu.CompilerParams(collective_id=cid, has_side_effects=True),
    )(a, b)


def compute(kernel, out, *args, flops=0):
    return pl.pallas_call(
        kernel,
        out_shape=out,
        compiler_params=pltpu.CompilerParams(vmem_limit_bytes=48 * 1024 * 1024),
        cost_estimate=pl.CostEstimate(
            flops=flops,
            bytes_accessed=sum(a.size * a.dtype.itemsize for a in args),
            transcendentals=0,
        ),
    )(*args)


def dot(a, b, dims=((1,), (0,)), precision=None):
    return lax.dot_general(
        a, b, (dims, ((), ())), precision=precision, preferred_element_type=F32
    )


def rms_scale(values):
    return lax.rsqrt(jnp.mean(values * values, axis=-1, keepdims=True) + EPSILON)


def rms_back(grad, values, scale, gain):
    weighted = grad * gain
    inner = jnp.mean(weighted * values, axis=-1, keepdims=True)
    return scale * weighted - values * (scale * scale * scale * inner)


def bucket_hot(buckets):
    return (lax.broadcasted_iota(jnp.int32, (BUCKETS, 512), 0) == buckets).astype(F32)


def attend_kernel(x, w, b, gain, table, buckets, normed_o, proj_o, probs_o, mixed_o, part_o):
    values = x[...].astype(F32).reshape(512, 768)
    normed = (values * rms_scale(values) * gain[...]).astype(BF)
    normed_o[...] = normed
    proj = dot(normed, w[:, :576]).astype(BF)
    proj_o[...] = proj
    by_offset = dot(table[...], bucket_hot(buckets[...]).astype(BF))
    seqs = [[], []]
    for h in range(3):
        line = jnp.broadcast_to(by_offset[h : h + 1], (256, 512))
        bias = pltpu.roll(line, 257, 1, stride=1, stride_axis=0)[:, :256]
        for s in range(2):
            rows = slice(256 * s, 256 * s + 256)
            query = proj[rows, 64 * h : 64 * h + 64]
            key = proj[rows, 192 + 64 * h : 256 + 64 * h]
            value = proj[rows, 384 + 64 * h : 448 + 64 * h]
            scores = dot(query, key, ((1,), (1,))) + bias
            exponent = jnp.exp(scores - jnp.max(scores, axis=-1, keepdims=True))
            probs = exponent / jnp.sum(exponent, axis=-1, keepdims=True)
            probs_o[3 * s + h] = probs
            seqs[s].append(dot(probs.astype(BF), value).astype(BF))
    mixed = jnp.concatenate([jnp.concatenate(s, axis=1) for s in seqs], axis=0)
    mixed_o[...] = mixed
    part_o[...] = dot(mixed, b[...]).astype(BF).reshape(4, 128, 768)


def route_kernel(
    x, parts, gain, router, routes, drop, cot, after_o, normed_o, probs_o, pick_o, send_o
):
    after = x[...].astype(F32) + jnp.sum(parts[...].astype(F32), axis=0)
    after_o[...] = after
    normed = (after * rms_scale(after) * gain[...]).astype(BF)
    normed_o[...] = normed
    logits = dot(normed, router[...])
    exponent = jnp.exp(logits - jnp.max(logits, axis=-1, keepdims=True))
    probs = exponent / jnp.sum(exponent, axis=-1, keepdims=True)
    probs_o[...] = probs
    chosen = routes[...]
    hot = chosen == lax.broadcasted_iota(jnp.int32, (128, EXPERTS), 1)
    gates = jnp.sum(jnp.where(hot, probs, 0.0), axis=-1, keepdims=True)
    kept = drop[...].astype(F32)
    grad_y = (cot[...].astype(F32) * (kept * gates)).astype(BF)
    earlier = lax.broadcasted_iota(jnp.int32, (128, 128), 1) < lax.broadcasted_iota(
        jnp.int32, (128, 128), 0
    )
    counts = dot(earlier.astype(F32).astype(BF), hot.astype(F32).astype(BF))
    slot = jnp.sum(jnp.where(hot, counts, 0.0), axis=-1, keepdims=True).astype(jnp.int32)
    place = jnp.where(drop[...] > 0, chosen * SLOT + slot, -SLOT)
    lanes = lax.broadcasted_iota(jnp.int32, (128, EXPERTS * SLOT), 1)
    pick = jnp.concatenate(
        [(lanes == place).astype(F32), (lanes == place + CAP).astype(F32)], axis=0
    ).astype(BF)
    pick_o[...] = pick
    both = jnp.concatenate([normed, grad_y], axis=0)
    send_o[...] = dot(pick, both, ((0,), (0,))).astype(BF).reshape(EXPERTS, SLOT, 768)


def compact_kernel(choose, x, out):
    flat = x[...].astype(F32).reshape(EXPERTS * SLOT, 768).astype(BF)
    out[...] = dot(choose[...], flat).astype(BF)


def expand_kernel(choose, x, out):
    total = jnp.sum(x[...].astype(F32), axis=0).astype(BF)
    out[...] = dot(choose[...], total, ((0,), (0,))).astype(BF).reshape(EXPERTS, SLOT, 768)


def add_kernel(x, out):
    out[...] = (x[0].astype(F32) + x[1].astype(F32)).astype(BF)


def expert_kernel(rows, w_in, w_out, parts, grad_in, grad_out):
    @pl.when(pl.program_id(0) == 0)
    def _():
        grad_in[...] = jnp.zeros_like(grad_in)
        grad_out[...] = jnp.zeros_like(grad_out)

    row = rows[:, 0].reshape(320, 768)
    grad = rows[:, 1].reshape(320, 768)
    pre = dot(row, w_in[...])
    square = pre * pre
    tanh = jnp.tanh(GELU_C * (pre + GELU_A * (pre * square)))
    half = 0.5 * (1.0 + tanh)
    act = (pre * half).astype(BF)
    slope = half + (0.5 * GELU_C) * pre * (1.0 - tanh * tanh) * (1.0 + 3.0 * GELU_A * square)
    parts[:, 0] = dot(act, w_out[...]).astype(BF).reshape(2, 160, 768)
    grad_act = dot(grad, w_out[...], ((1,), (1,)))
    grad_pre = (grad_act * slope).astype(BF)
    parts[:, 1] = dot(grad_pre, w_in[...], ((1,), (1,))).astype(BF).reshape(2, 160, 768)
    grad_in[...] += dot(row, grad_pre, ((0,), (0,)))
    grad_out[...] += dot(act, grad, ((0,), (0,)))


def experts(rows, w_in, w_out):
    block = pl.BlockSpec((2, 2, 160, 768), lambda i: (i, 0, 0, 0))
    whole_in = pl.BlockSpec((768, 384), lambda i: (0, 0))
    whole_out = pl.BlockSpec((384, 768), lambda i: (0, 0))
    return pl.pallas_call(
        expert_kernel,
        grid=(4,),
        out_shape=[
            jax.ShapeDtypeStruct((8, 2, 160, 768), BF),
            jax.ShapeDtypeStruct((768, 384), F32),
            jax.ShapeDtypeStruct((384, 768), F32),
        ],
        in_specs=[block, whole_in, whole_out],
        out_specs=[block, whole_in, whole_out],
        compiler_params=pltpu.CompilerParams(vmem_limit_bytes=48 * 1024 * 1024),
        cost_estimate=pl.CostEstimate(
            flops=12 * 1280 * 768 * 384, bytes_accessed=12000000, transcendentals=0
        ),
    )(rows, w_in, w_out)


def after_kernel(
    back,
    pick,
    after,
    normed,
    probs,
    routes,
    drop,
    cot,
    gain,
    router,
    result_o,
    grad_after_o,
    grad_low_o,
    grad_router_o,
    grad_gain_o,
):
    flat = back[...].astype(F32).reshape(EXPERTS * SLOT, 768).astype(BF)
    expert_y = dot(pick[:128], flat)
    slot_grad = dot(pick[128:], flat)
    hot = routes[...] == lax.broadcasted_iota(jnp.int32, (128, EXPERTS), 1)
    gates = jnp.sum(jnp.where(hot, probs[...], 0.0), axis=-1, keepdims=True)
    kept = drop[...].astype(F32)
    values = after[...]
    result_o[...] = (values + (kept * gates) * expert_y).astype(BF)
    grad = cot[...].astype(F32)
    grad_gate = kept * jnp.sum(grad * expert_y, axis=-1, keepdims=True)
    grad_logits = ((grad_gate * gates) * (hot.astype(F32) - probs[...])).astype(BF)
    grad_router_o[...] = dot(normed[...], grad_logits, ((0,), (0,)))
    grad_normed = dot(grad_logits, router[...], ((1,), (1,))) + slot_grad
    scale = rms_scale(values)
    grad_gain_o[...] = jnp.sum(grad_normed * values * scale, axis=0, keepdims=True)
    grad_after = grad + rms_back(grad_normed, values, scale, gain[...])
    grad_after_o[...] = grad_after
    grad_low_o[...] = grad_after.astype(BF)


def attend_back_kernel(
    x,
    normed,
    proj,
    probs,
    mixed,
    grad_proj,
    w,
    b,
    buckets,
    grad_qkv_o,
    grad_out_o,
    part_o,
    grad_gain_o,
    grad_table_o,
):
    values = x[...].astype(F32).reshape(512, 768)
    grad_in = grad_proj[...].reshape(512, 768)
    grad_mixed = dot(grad_in, b[...], ((1,), (1,))).astype(BF)
    grad_out_o[...] = dot(mixed[...], grad_in, ((0,), (0,))).astype(BF).reshape(8, 24, 768)
    flip = (
        lax.broadcasted_iota(jnp.int32, (256, 256), 0)
        + lax.broadcasted_iota(jnp.int32, (256, 256), 1)
        == 255
    )
    flip = flip.astype(F32).astype(BF)
    pieces = [[[], [], []], [[], [], []]]
    sums = []
    for h in range(3):
        turned = jnp.zeros((256, 256), F32)
        for s in range(2):
            rows = slice(256 * s, 256 * s + 256)
            query = proj[rows, 64 * h : 64 * h + 64]
            key = proj[rows, 192 + 64 * h : 256 + 64 * h]
            value = proj[rows, 384 + 64 * h : 448 + 64 * h]
            grad_rows = grad_mixed[rows, 64 * h : 64 * h + 64]
            weights = probs[3 * s + h]
            grad_probs = dot(grad_rows, value, ((1,), (1,)))
            inner = jnp.sum(weights * grad_probs, axis=-1, keepdims=True)
            grad_scores = (weights * (grad_probs - inner)).astype(BF)
            turned = turned + dot(flip, grad_scores)
            pieces[s][0].append(dot(grad_scores, key).astype(BF))
            pieces[s][1].append(dot(grad_scores, query, ((0,), (0,))).astype(BF))
            pieces[s][2].append(dot(weights.astype(BF), grad_rows, ((0,), (0,))).astype(BF))
        wide = jnp.concatenate([turned, jnp.zeros((256, 256), F32)], axis=1)
        wide = pltpu.roll(wide, 0, 1, stride=1, stride_axis=0)
        sums.append(jnp.sum(wide, axis=0, keepdims=True))
    sums = jnp.concatenate(sums + [jnp.zeros((5, 512), F32)], axis=0)
    grad_table_o[...] = dot(
        sums, bucket_hot(buckets[...]), ((1,), (1,)), precision=lax.Precision.HIGHEST
    )
    grad_qkv = jnp.concatenate(
        [jnp.concatenate([p for part in s for p in part], axis=1) for s in pieces], axis=0
    )
    grad_qkv_o[...] = dot(normed[...], grad_qkv, ((0,), (0,)))
    grad_normed = dot(grad_qkv, w[:, :576], ((1,), (1,)))
    part_o[...] = grad_normed.astype(BF).reshape(4, 128, 768)
    grad_gain_o[...] = jnp.sum(grad_normed * values * rms_scale(values), axis=0, keepdims=True)


def finish_kernel(x, parts, grad_after, gain, out):
    values = x[...].astype(F32)
    grad_normed = jnp.sum(parts[...].astype(F32), axis=0)
    out[...] = (
        grad_after[...] + rms_back(grad_normed, values, rms_scale(values), gain[...])
    ).astype(BF)


def sum_kernel(a, b, a_o, b_o):
    a_o[...] = jnp.sum(a[...].astype(F32), axis=0)
    b_o[...] = jnp.sum(b[...].astype(F32), axis=0)


def choose_matrix():
    choose = np.zeros((2 * EXPERTS * CAP, EXPERTS * SLOT), np.float32)
    for kind in range(2):
        for source in range(EXPERTS):
            for slot in range(CAP):
                choose[
                    kind * EXPERTS * CAP + source * CAP + slot, source * SLOT + kind * CAP + slot
                ] = 1.0
    return choose


def shape(*dims, dtype=BF):
    return jax.ShapeDtypeStruct(dims, dtype)


def body(
    inputs,
    cotangent,
    routes,
    drop_mask,
    buckets,
    qkv_weight,
    out_weight,
    router_weight,
    attn_gain,
    ffn_gain,
    bias_table,
    expert_in,
    expert_out,
):
    f = flat_id()
    m, g = f % 4, f // 4
    plane = g // 8
    choose = jnp.asarray(choose_matrix(), BF)
    offsets = jnp.pad(buckets, (0, 1), constant_values=-1).reshape(1, 512)
    drop = drop_mask.reshape(128, 1)

    quarters = qkv_weight.reshape(6, 3, 4, 192).transpose(2, 0, 1, 3).reshape(4, 6, 576)
    small = jnp.concatenate(
        [
            router_weight,
            attn_gain[:, None],
            ffn_gain[:, None],
            jnp.pad(bias_table, (0, 3))[:, None],
            jnp.zeros((6, 45), BF),
        ],
        axis=1,
    )
    packed = jnp.concatenate([quarters, jnp.broadcast_to(small, (4, 6, 64))], axis=2)
    packed = jnp.pad(packed, ((0, 0), (0, 10), (0, 0)))
    tokens, packed, out_rows = exchange(
        0, QUAD, (inputs, True), (packed, False), (jnp.pad(out_weight, ((0, 10), (0, 0))), True)
    )
    wide, out_mine = gather_weights(
        1, packed[:, :6].reshape(24, 640), out_rows[:, :6].reshape(24, 768)
    )
    weights = wide.reshape(768, 640)
    out_mine = out_mine.reshape(192, 768)
    router = weights[:, 576:592]
    gains = weights[:, 592:594].astype(F32).T
    gain_one, gain_two = gains[0:1], gains[1:2]
    table = wide[:, :, 594].reshape(BUCKETS, 4, 6)[:, :, :3]
    table = lax.dynamic_index_in_dim(table, m, 1, keepdims=False).T
    table = jnp.pad(table, ((0, 5), (0, 0)))

    normed, proj, probs, mixed, parts = compute(
        attend_kernel,
        [
            shape(512, 768),
            shape(512, 576),
            shape(6, 256, 256, dtype=F32),
            shape(512, 192),
            shape(4, 128, 768),
        ],
        tokens,
        weights,
        out_mine,
        gain_one,
        table,
        offsets,
    )
    (parts,) = exchange(2, QUAD, (parts, False))
    after, normed_two, router_probs, pick, send = compute(
        route_kernel,
        [
            shape(128, 768, dtype=F32),
            shape(128, 768),
            shape(128, EXPERTS, dtype=F32),
            shape(256, EXPERTS * SLOT),
            shape(EXPERTS, SLOT, 768),
        ],
        inputs,
        parts,
        gain_two,
        router,
        routes,
        drop,
        cotangent,
    )
    (arrived,) = exchange(3, SAME_R, (send, False))
    rows = compute(compact_kernel, shape(320, 768), choose, arrived)
    (rows,) = exchange(4, PLANE, (rows, True))
    (rows,) = exchange(5, MATE, (rows, True))
    parts, grad_expert_in, grad_expert_out = experts(
        rows.reshape(8, 2, 160, 768), expert_in, expert_out
    )
    (parts,) = exchange(6, MATE, (parts.reshape(2, 4, 320, 768), False))
    parts = compute(add_kernel, shape(4, 320, 768), parts)
    (parts,) = exchange(7, PLANE, (parts, False))
    back = compute(expand_kernel, shape(EXPERTS, SLOT, 768), choose, parts)
    (back,) = exchange(8, SAME_R, (back, False))
    result, grad_after, grad_low, grad_router, grad_gain_two = compute(
        after_kernel,
        [
            shape(128, 768),
            shape(128, 768, dtype=F32),
            shape(128, 768),
            shape(768, EXPERTS, dtype=F32),
            shape(1, 768, dtype=F32),
        ],
        back,
        pick,
        after,
        normed_two,
        router_probs,
        routes,
        drop,
        cotangent,
        gain_two,
        router,
    )
    (grad_proj,) = exchange(9, QUAD, (grad_low, True))
    grad_qkv, grad_out, parts, grad_gain_one, grad_table = compute(
        attend_back_kernel,
        [
            shape(768, 576, dtype=F32),
            shape(8, 24, 768),
            shape(4, 128, 768),
            shape(1, 768, dtype=F32),
            shape(8, BUCKETS, dtype=F32),
        ],
        tokens,
        normed,
        proj,
        probs,
        mixed,
        grad_proj,
        weights,
        out_mine,
        offsets,
    )
    grad_bias = lax.dynamic_update_slice(
        jnp.zeros((BUCKETS, 4, 6), F32), grad_table[:3].T.reshape(BUCKETS, 1, 3), (0, m, 0)
    )
    grad_wide = jnp.concatenate(
        [
            grad_qkv,
            grad_router,
            grad_gain_one.T,
            grad_gain_two.T,
            grad_bias.reshape(768, 1),
            jnp.zeros((768, 45), F32),
        ],
        axis=1,
    ).astype(BF)
    (parts,) = exchange(10, QUAD, (parts, False))
    grad_input = compute(
        finish_kernel, shape(128, 768), inputs, parts, grad_after, gain_one
    )
    got_wide, got_out = scatter_grads(11, grad_wide.reshape(32, 24, 640), grad_out)
    sum_wide, sum_out = compute(
        sum_kernel, [shape(24, 640, dtype=F32), shape(24, 768, dtype=F32)], got_wide, got_out
    )
    final = jnp.concatenate([sum_wide, sum_out], axis=1).reshape(4, 6, 1408)
    (final,) = exchange(12, QUAD, (jnp.pad(final, ((0, 0), (0, 2), (0, 0))), False))
    final = final[:, :6]
    small = jnp.sum(final[:, :, 576:640], axis=0)
    grad_qkv = final[:, :, :576].reshape(4, 6, 3, 192).transpose(1, 2, 0, 3).reshape(6, 2304)
    grad_out = lax.dynamic_index_in_dim(final[:, :, 640:], plane, 0, keepdims=False)
    return (
        result,
        grad_input,
        grad_qkv,
        grad_out,
        small[:, :16],
        small[:, 16],
        small[:, 17],
        small[:3, 18],
        grad_expert_in,
        grad_expert_out,
    )


def solution(mesh):
    placed = (
        P(("fsdp", "sp"), None),
        P(("fsdp", "sp"), None),
        P(("fsdp", "sp"), None),
        P(("fsdp", "sp")),
        P(),
        P(("fsdp", "sp"), None),
        P(("fsdp", "sp"), None),
        P(("fsdp", "sp"), None),
        P(("fsdp", "sp")),
        P(("fsdp", "sp")),
        P(("fsdp", "sp")),
        P(None, ("fsdp", "sp")),
        P(("fsdp", "sp"), None),
    )
    return jax.shard_map(
        body,
        mesh=mesh,
        in_specs=placed,
        out_specs=(
            P(("fsdp", "sp"), None),
            P(("fsdp", "sp"), None),
            P(("fsdp", "sp"), None),
            P(("fsdp", "sp"), None),
            P(("fsdp", "sp"), None),
            P(("fsdp", "sp")),
            P(("fsdp", "sp")),
            P(("fsdp", "sp")),
            P(None, ("fsdp", "sp")),
            P(("fsdp", "sp"), None),
        ),
        check_vma=False,
    )
```

```python
import functools

import jax
import jax.numpy as jnp
import numpy as np
from jax import lax
from jax.experimental import pallas as pl
from jax.experimental.pallas import tpu as pltpu
from jax.sharding import PartitionSpec as P

HEADS = 12
HEAD_DIM = 64
EXPERTS = 16
BUCKETS = 32
CAP = 10
EPSILON = 1e-06
MESH = pl.DeviceIdType.MESH
BF = jnp.bfloat16
F32 = jnp.float32
SLOT = 24
GELU_C = 0.7978845608028654
GELU_A = 0.044715
DEPTH = 2 * EXPERTS * CAP
HALF = EXPERTS * CAP


def coords(flat):
    return (lax.div(flat, 2), lax.rem(flat, 2))


def for_range(low, high, fn):
    def step(j, carry):
        fn(j)
        return carry

    lax.fori_loop(low, high, step, 0)


def dot(a, b, dims=((1,), (0,)), precision=None):
    return lax.dot_general(
        a, b, (dims, ((), ())), precision=precision, preferred_element_type=F32
    )


def rms_scale(values):
    return lax.rsqrt(jnp.mean(values * values, axis=-1, keepdims=True) + EPSILON)


def rms_back(grad, values, scale, gain):
    weighted = grad * gain
    inner = jnp.mean(weighted * values, axis=-1, keepdims=True)
    return scale * weighted - values * (scale * scale * scale * inner)


def iota(shape, dim):
    return lax.broadcasted_iota(jnp.int32, shape, dim)


def ones_where(mask):
    return mask.astype(F32).astype(BF)


class Links:
    def __init__(self, send, recv):
        self.send, self.recv, self.used = send, recv, 0

    def pair(self, count=1):
        first = self.used
        self.used += count
        return first

    def copy(self, index, source, target, device):
        return pltpu.make_async_remote_copy(
            src_ref=source,
            dst_ref=target,
            send_sem=self.send.at[index],
            recv_sem=self.recv.at[index],
            device_id=coords(device),
            device_id_type=MESH,
        )


def rows_of(ref):
    blocks, rows, width = ref.shape
    return ref[...].astype(F32).reshape(blocks * rows, width).astype(BF)


def layer_kernel(
    x,
    routes,
    drop,
    buckets,
    qkv,
    out_w,
    router_w,
    gain_attn,
    gain_ffn,
    bias_w,
    cot_any,
    expert_in_any,
    expert_out_any,
    choose_any,
    grad_input_o,
    grad_qkv_o,
    grad_out_o,
    grad_small_o,
    result_any,
    grad_in_any,
    grad_eout_any,
    cot,
    expert_in,
    expert_out,
    choose,
    result_s,
    grad_in_o,
    grad_eout_o,
    offsets,
    lines_s,
    packs,
    packs_in,
    rawb,
    rawb_in,
    lay_a,
    lay_b,
    chunk_a,
    chunk_b,
    wide,
    weights_s,
    outs,
    tokens,
    normed_s,
    proj_s,
    probs_s,
    mixed_s,
    part,
    from_mate,
    merge,
    to_x,
    from_x,
    after_s,
    normed_two_s,
    send_s,
    arrived,
    rows_s,
    parts_s,
    mate_parts,
    sums_s,
    got_x,
    got_z,
    diag_x,
    diag_z,
    back_s,
    back_in,
    grad_after_s,
    grad_low,
    grad_wide,
    grad_wide_in,
    grad_out_s,
    grad_out_in,
    fin,
    fin_in,
    send_sem,
    recv_sem,
    local_sem,
):
    loads = [
        pltpu.make_async_copy(source, target, local_sem.at[i])
        for i, (source, target) in enumerate(
            [
                (cot_any, cot),
                (expert_in_any, expert_in),
                (expert_out_any, expert_out),
                (choose_any, choose),
            ]
        )
    ]
    stores = [
        pltpu.make_async_copy(source, target, local_sem.at[4 + i])
        for i, (source, target) in enumerate(
            [(result_s, result_any), (grad_in_o, grad_in_any), (grad_eout_o, grad_eout_any)]
        )
    ]
    links = Links(send_sem, recv_sem)
    fs, sp = lax.axis_index("fsdp"), lax.axis_index("sp")
    f = fs * 2 + sp
    m, g = lax.rem(f, 4), lax.div(f, 4)
    plane, place = lax.div(g, 8), lax.rem(g, 8)
    core, x_lo = lax.div(m, 2), lax.rem(m, 2)
    expert, member = lax.div(f, 8), lax.rem(f, 8)
    z_lo = lax.div(member, 4)
    quad = f - m
    mate_m = (1 - core) * 2 + x_lo
    beside_m = core * 2 + (1 - x_lo)
    cross_m = (1 - core) * 2 + (1 - x_lo)
    mate, beside = quad + mate_m, quad + beside_m
    above = f - z_lo * 4 + (1 - z_lo) * 4
    spot = z_lo * 2 + x_lo
    spot_x = z_lo * 2 + (1 - x_lo)
    spot_z = (1 - z_lo) * 2 + x_lo
    spot_d = (1 - z_lo) * 2 + (1 - x_lo)

    barrier = pltpu.get_barrier_semaphore()

    def hello(device):
        pl.semaphore_signal(barrier, inc=1, device_id=coords(device), device_id_type=MESH)

    for j in range(1, 4):
        hello(quad + lax.rem(m + j, 4))
    for_range(1, 32, lambda j: hello(4 * lax.rem(g + j, 32) + m))

    for load in loads:
        load.start()
    tokens[m] = x[...]
    offsets[...] = jnp.full((1, 512), -1, jnp.int32)
    offsets[:, :511] = buckets[...]
    lines_s[...] = jnp.zeros((8, 128), F32)
    lines_s[0:1, 0:6] = gain_attn[...].astype(F32)
    lines_s[1:2, 0:6] = gain_ffn[...].astype(F32)
    lines_s[2:3, 0:3] = bias_w[...].astype(F32)
    lines_s[3:4] = routes[...].astype(F32)
    lines_s[4:5] = drop[...].astype(F32)
    columns_of = lines_s[...].T
    chosen = columns_of[:, 3:4].astype(jnp.int32)
    kept = columns_of[:, 4:5]
    weight = qkv[...].astype(F32)
    extra = jnp.concatenate(
        [router_w[...].astype(F32), columns_of[:6], jnp.zeros((6, 40), F32)], axis=1
    )
    for k in range(4):
        columns = [weight[:, 768 * i + 192 * k : 768 * i + 192 * k + 192] for i in range(3)]
        packs[k, 0:6] = jnp.concatenate(columns + [extra], axis=1).astype(BF)
    rawb[0:6] = out_w[...]
    pl.semaphore_wait(barrier, 34)

    base_p, base_b = links.pair(4), links.pair(4)

    def copy_pack(j):
        k = lax.rem(m + j, 4)
        return links.copy(base_p + j, packs.at[k], packs_in.at[m], quad + k)

    def copy_raw(j):
        return links.copy(base_b + j, rawb, rawb_in.at[m], quad + lax.rem(m + j, 4))

    for j in range(1, 4):
        copy_pack(j).start()
        copy_raw(j).start()
    packs_in[m] = packs[m]
    rawb_in[m] = rawb[...]

    def gather_four(buffer):
        first = links.pair(3)
        to_mate = links.copy(first, buffer.at[m], buffer.at[m], mate)
        to_beside = links.copy(first + 1, buffer.at[m], buffer.at[m], beside)
        passed = links.copy(first + 2, buffer.at[beside_m], buffer.at[beside_m], mate)
        return to_mate, to_beside, passed

    def finish_four(copies):
        to_mate, to_beside, passed = copies
        to_beside.wait_recv()
        passed.start()
        to_mate.wait()
        to_beside.wait_send()
        passed.wait()

    token_copies = gather_four(tokens)
    token_copies[1].start()
    token_copies[0].start()
    for j in range(1, 4):
        copy_pack(j).wait()
        copy_raw(j).wait()
    for k in range(4):
        lay_a[6 * k : 6 * k + 6] = packs_in[k].astype(F32)[0:6]
        lay_b[6 * k : 6 * k + 6] = rawb_in[k].astype(F32)[0:6]
    chunk_a[...] = lay_a[...].astype(BF)
    chunk_b[...] = lay_b[...].astype(BF)

    base_a = links.pair(32)
    base_o, base_r = links.pair(32), links.pair(8)

    def copy_a(j):
        return links.copy(base_a + j, chunk_a, wide.at[g], 4 * lax.rem(g + j, 32) + m)

    def copy_b(j, q):
        return pltpu.make_async_remote_copy(
            src_ref=chunk_b,
            dst_ref=outs.at[q],
            send_sem=send_sem.at[base_o + j],
            recv_sem=recv_sem.at[base_r + q],
            device_id=coords(4 * lax.rem(g + j, 32) + m),
            device_id_type=MESH,
        )

    for_range(1, 32, lambda j: copy_a(j).start())

    @pl.when(plane == m)
    def _():
        for_range(1, 32, lambda j: copy_b(j, place).start())
        outs[place] = chunk_b[...]

    wide[g] = chunk_a[...]
    finish_four(token_copies)
    values = tokens[...].astype(F32).reshape(512, 768)
    scaled = values * rms_scale(values)
    for_range(1, 32, lambda j: copy_a(j).wait())

    weights_s[...] = rows_of(wide)
    weights = weights_s[...]
    turned = weights[:, 512:640].astype(F32).T
    gain_one, gain_two, table = turned[80:81], turned[81:82], turned[82:83]
    router = weights[:, 576:592]
    bucket = offsets[...]
    head_row = (iota((32, 24, 128), 1).reshape(768, 128) == 6 * m + iota((768, 128), 1)).astype(F32)
    head_row = head_row.T[:8]
    head_row = jnp.where(iota((8, 768), 0) < 3, head_row, 0.0)
    in_bucket = iota((32, 24, 512), 0).reshape(768, 512) == bucket
    by_offset = dot((head_row * table).astype(BF), ones_where(in_bucket))
    normed = (scaled * gain_one).astype(BF)
    normed_s[...] = normed
    proj = dot(normed, weights[:, :576]).astype(BF)
    proj_s[...] = proj
    seqs = [[], []]
    for h in range(3):
        line = jnp.broadcast_to(by_offset[h : h + 1], (256, 512))
        bias = pltpu.roll(line, 257, 1, stride=1, stride_axis=0)[:, :256]
        for s in range(2):
            rows = slice(256 * s, 256 * s + 256)
            query = proj[rows, 64 * h : 64 * h + 64]
            key = proj[rows, 192 + 64 * h : 256 + 64 * h]
            value = proj[rows, 384 + 64 * h : 448 + 64 * h]
            scores = dot(query, key, ((1,), (1,))) + bias
            exponent = jnp.exp(scores - jnp.max(scores, axis=-1, keepdims=True))
            probs = exponent / jnp.sum(exponent, axis=-1, keepdims=True)
            probs_s[3 * s + h] = probs
            seqs[s].append(dot(probs.astype(BF), value).astype(BF))
    mixed = jnp.concatenate([jnp.concatenate(s, axis=1) for s in seqs], axis=0)
    mixed_s[...] = mixed

    def take_b(q):
        @pl.when(8 * m + q != g)
        def _():
            copy_b(1, q).wait_recv()

    for_range(0, 8, take_b)

    @pl.when(plane == m)
    def _():
        for_range(1, 32, lambda j: copy_b(j, place).wait_send())

    out_mine = rows_of(outs)
    part[0] = dot(mixed, out_mine).astype(BF).reshape(4, 128, 768)

    def reduce_start(n):
        first = links.pair(3)
        cross = links.copy(first, part.at[n, cross_m], merge.at[n], mate)
        straight = links.copy(first + 1, part.at[n, mate_m], from_mate.at[n], mate)
        over = links.copy(first + 2, to_x.at[n], from_x.at[n], beside)
        cross.start()
        straight.start()
        return cross, straight, over

    def reduce_pass(n, copies):
        cross, straight, over = copies
        cross.wait()
        to_x[n] = (part[n, beside_m].astype(F32) + merge[n].astype(F32)).astype(BF)
        over.start()

    def reduce_end(n, copies):
        cross, straight, over = copies
        straight.wait()
        over.wait()
        return part[n, m].astype(F32) + from_mate[n].astype(F32) + from_x[n].astype(F32)

    copies = reduce_start(0)
    reduce_pass(0, copies)
    hot = chosen == iota((128, EXPERTS), 1)
    earlier = iota((128, 128), 1) < iota((128, 128), 0)
    counts = dot(ones_where(earlier), ones_where(hot))
    slot = jnp.sum(jnp.where(hot, counts, 0.0), axis=-1, keepdims=True).astype(jnp.int32)
    target = jnp.where(kept > 0, chosen * SLOT + slot, -SLOT)
    lanes = iota((128, EXPERTS * SLOT), 1)
    pick_row, pick_grad = ones_where(lanes == target), ones_where(lanes == target + CAP)
    loads[0].wait()
    grad = cot[...].astype(F32)
    after = x[...].astype(F32) + reduce_end(0, copies)
    after_s[...] = after
    normed_two = (after * rms_scale(after) * gain_two).astype(BF)
    normed_two_s[...] = normed_two
    logits = dot(normed_two, router)
    exponent = jnp.exp(logits - jnp.max(logits, axis=-1, keepdims=True))
    router_probs = exponent / jnp.sum(exponent, axis=-1, keepdims=True)
    gates = jnp.sum(jnp.where(hot, router_probs, 0.0), axis=-1, keepdims=True)
    grad_y = (grad * (kept * gates)).astype(BF)
    slots = dot(
        jnp.concatenate([pick_row, pick_grad], axis=0),
        jnp.concatenate([normed_two, grad_y], axis=0),
        ((0,), (0,)),
    )
    send_s[...] = slots.astype(BF).reshape(EXPERTS, SLOT, 768)

    def spread(source, target, base):
        def copy(j):
            k = lax.rem(expert + j, EXPERTS)
            return links.copy(base + j, source.at[k], target.at[expert], 8 * k + member)

        return copy

    copy_d = spread(send_s, arrived, links.pair(EXPERTS))
    for_range(1, EXPERTS, lambda j: copy_d(j).start())
    arrived[expert] = send_s[expert]
    grad_in_o[...] = jnp.zeros_like(grad_in_o)
    grad_eout_o[...] = jnp.zeros_like(grad_eout_o)
    for_range(1, EXPERTS, lambda j: copy_d(j).wait())
    loads[3].wait()
    rows_s[spot, core] = dot(choose[...], rows_of(arrived)).astype(BF)
    first_half, second_half = pl.ds(0, HALF), pl.ds(HALF, HALF)

    def rows_copy(place_of, half, device):
        ref = rows_s.at[place_of, core, half]
        return links.copy(links.pair(), ref, ref, device)

    out_x2 = rows_copy(spot, second_half, beside)
    out_z1 = rows_copy(spot, first_half, above)
    out_x1 = rows_copy(spot, first_half, beside)
    out_z2 = rows_copy(spot, second_half, above)
    out_m1 = rows_copy(spot, first_half, mate)
    out_m2 = rows_copy(spot, second_half, mate)
    pass_x = rows_copy(spot_z, first_half, beside)
    pass_z = rows_copy(spot_x, second_half, above)
    mate_x1, mate_x2 = (rows_copy(spot_x, h, mate) for h in (first_half, second_half))
    mate_z1, mate_z2 = (rows_copy(spot_z, h, mate) for h in (first_half, second_half))
    mate_d1, mate_d2 = (rows_copy(spot_d, h, mate) for h in (first_half, second_half))
    for copy in (out_x2, out_z1, out_m1, out_m2, out_x1, out_z2):
        copy.start()

    def expert_step(place_of):
        def to_mate(half):
            copy = links.copy(
                links.pair(),
                parts_s.at[place_of, 1 - core, half],
                mate_parts.at[place_of, half],
                mate,
            )
            copy.start()
            return copy

        both = rows_s[place_of]
        row = both[:, :HALF].reshape(DEPTH, 768)
        grad_row = both[:, HALF:].reshape(DEPTH, 768)
        pre = dot(row, expert_in[...])
        square = pre * pre
        tanh = jnp.tanh(GELU_C * (pre + GELU_A * (pre * square)))
        half = 0.5 * (1.0 + tanh)
        act = (pre * half).astype(BF)
        slope = half + (0.5 * GELU_C) * pre * (1.0 - tanh * tanh) * (1.0 + 3.0 * GELU_A * square)
        parts_s[place_of, :, :HALF] = dot(act, expert_out[...]).astype(BF).reshape(2, HALF, 768)
        one = to_mate(first_half)
        grad_act = dot(grad_row, expert_out[...], ((1,), (1,)))
        grad_pre = (grad_act * slope).astype(BF)
        parts_s[place_of, :, HALF:] = (
            dot(grad_pre, expert_in[...], ((1,), (1,))).astype(BF).reshape(2, HALF, 768)
        )
        two = to_mate(second_half)
        grad_in_o[...] += dot(row, grad_pre, ((0,), (0,)))
        grad_eout_o[...] += dot(act, grad_row, ((0,), (0,)))
        one.wait()
        two.wait()
        sums_s[place_of] = (
            parts_s[place_of, core].astype(F32) + mate_parts[place_of].astype(F32)
        ).astype(BF)

    def sums_copy(place_of, half, target, device):
        copy = links.copy(links.pair(), sums_s.at[place_of, half], target, device)
        copy.start()
        return copy

    loads[1].wait()
    loads[2].wait()
    out_m1.wait()
    out_m2.wait()
    expert_step(spot)
    out_x2.wait()
    pass_z.start()
    mate_x2.start()
    out_z1.wait()
    pass_x.start()
    mate_z1.start()
    out_x1.wait()
    mate_x1.start()
    out_z2.wait()
    mate_z2.start()
    mate_x2.wait()
    mate_x1.wait()
    expert_step(spot_x)
    x_one = sums_copy(spot_x, first_half, got_x.at[first_half], beside)
    pass_z.wait()
    mate_d2.start()
    pass_x.wait()
    mate_d1.start()
    mate_z1.wait()
    mate_z2.wait()
    expert_step(spot_z)
    z_two = sums_copy(spot_z, second_half, got_z.at[second_half], above)
    mate_d1.wait()
    mate_d2.wait()
    expert_step(spot_d)
    d_one = sums_copy(spot_d, first_half, diag_x, beside)
    d_two = sums_copy(spot_d, second_half, diag_z, above)
    stores[1].start()
    stores[2].start()
    d_one.wait()
    sums_s[spot_z, :HALF] = (sums_s[spot_z, :HALF].astype(F32) + diag_x[...].astype(F32)).astype(
        BF
    )
    z_one = sums_copy(spot_z, first_half, got_z.at[first_half], above)
    d_two.wait()
    sums_s[spot_x, HALF:] = (sums_s[spot_x, HALF:].astype(F32) + diag_z[...].astype(F32)).astype(
        BF
    )
    x_two = sums_copy(spot_x, second_half, got_x.at[second_half], beside)
    for copy in (x_one, z_two, z_one, x_two):
        copy.wait()
    total = sums_s[spot].astype(F32) + got_x[...].astype(F32) + got_z[...].astype(F32)
    back_s[...] = (
        dot(choose[...], total.astype(BF), ((0,), (0,))).astype(BF).reshape(EXPERTS, SLOT, 768)
    )
    copy_r = spread(back_s, back_in, links.pair(EXPERTS))
    for_range(1, EXPERTS, lambda j: copy_r(j).start())
    back_in[expert] = back_s[expert]
    for_range(1, EXPERTS, lambda j: copy_r(j).wait())

    flat = rows_of(back_in)
    expert_y = dot(pick_row, flat)
    slot_grad = dot(pick_grad, flat)
    after = after_s[...]
    grad_gate = kept * jnp.sum(grad * expert_y, axis=-1, keepdims=True)
    grad_logits = ((grad_gate * gates) * (hot.astype(F32) - router_probs)).astype(BF)
    grad_normed = dot(grad_logits, router, ((1,), (1,))) + slot_grad
    scale = rms_scale(after)
    grad_after = grad + rms_back(grad_normed, after, scale, gain_two)
    grad_after_s[...] = grad_after
    grad_low[m] = grad_after.astype(BF)
    low_copies = gather_four(grad_low)
    low_copies[1].start()
    low_copies[0].start()
    result_s[...] = (after + (kept * gates) * expert_y).astype(BF)
    stores[0].start()
    grad_router = dot(grad_logits, normed_two_s[...], ((0,), (0,)))
    grad_gain_two = jnp.sum(grad_normed * after * scale, axis=0, keepdims=True)
    finish_four(low_copies)

    grad_proj = grad_low[...].reshape(512, 768)
    grad_mixed = dot(grad_proj, out_mine, ((1,), (1,))).astype(BF)
    grad_out = dot(mixed_s[...], grad_proj, ((0,), (0,)))
    grad_out_s[...] = grad_out.astype(BF).reshape(8, 24, 768)
    base_gs, base_gr = links.pair(8), links.pair(32)

    def copy_go(q):
        p = 8 * m + q
        return pltpu.make_async_remote_copy(
            src_ref=grad_out_s.at[q],
            dst_ref=grad_out_in.at[g],
            send_sem=send_sem.at[base_gs + q],
            recv_sem=recv_sem.at[base_gr + lax.rem(p - g + 32, 32)],
            device_id=coords(4 * p + m),
            device_id_type=MESH,
        )

    def away(q, fn):
        @pl.when(8 * m + q != g)
        def _():
            fn(q)

    for_range(0, 8, lambda q: away(q, lambda k: copy_go(k).start()))
    flip = ones_where(iota((256, 256), 0) + iota((256, 256), 1) == 255)
    pieces = [[[], [], []], [[], [], []]]
    sums = []
    for h in range(3):
        mirrored = jnp.zeros((256, 256), F32)
        for s in range(2):
            rows = slice(256 * s, 256 * s + 256)
            query = proj_s[rows, 64 * h : 64 * h + 64]
            key = proj_s[rows, 192 + 64 * h : 256 + 64 * h]
            value = proj_s[rows, 384 + 64 * h : 448 + 64 * h]
            grad_rows = grad_mixed[rows, 64 * h : 64 * h + 64]
            probs = probs_s[3 * s + h]
            grad_probs = dot(grad_rows, value, ((1,), (1,)))
            inner = jnp.sum(probs * grad_probs, axis=-1, keepdims=True)
            grad_scores = (probs * (grad_probs - inner)).astype(BF)
            mirrored = mirrored + dot(flip, grad_scores)
            pieces[s][0].append(dot(grad_scores, key).astype(BF))
            pieces[s][1].append(dot(grad_scores, query, ((0,), (0,))).astype(BF))
            pieces[s][2].append(dot(probs.astype(BF), grad_rows, ((0,), (0,))).astype(BF))
        line = jnp.concatenate([mirrored, jnp.zeros((256, 256), F32)], axis=1)
        line = pltpu.roll(line, 0, 1, stride=1, stride_axis=0)
        sums.append(jnp.sum(line, axis=0, keepdims=True))
    grad_heads = jnp.concatenate(
        [jnp.concatenate([p for part_of in s for p in part_of], axis=1) for s in pieces], axis=0
    )
    sums = jnp.concatenate(sums + [jnp.zeros((5, 512), F32)], axis=0)
    high = sums.astype(BF)
    rest = sums - high.astype(F32)
    middle = rest.astype(BF)
    low = (rest - middle.astype(F32)).astype(BF)
    in_bucket = iota((32, 24, 512), 0).reshape(768, 512) == offsets[...]
    grad_table = dot(
        jnp.concatenate([high.astype(F32), middle.astype(F32), low.astype(F32)], axis=0).astype(BF),
        ones_where(in_bucket),
        ((1,), (1,)),
    )
    grad_table = (grad_table[16:24] + grad_table[8:16]) + grad_table[0:8]
    grad_table = jnp.sum(grad_table * head_row, axis=0, keepdims=True)
    lines = jnp.concatenate(
        [
            grad_router,
            jnp.zeros((1, 768), F32),
            grad_gain_two,
            grad_table,
            jnp.zeros((45, 768), F32),
        ],
        axis=0,
    )
    grad_qkv = dot(normed_s[...], grad_heads, ((0,), (0,)))
    grad_wide[...] = (
        jnp.concatenate([grad_qkv, lines.T], axis=1).reshape(32, 24, 640).astype(BF)
    )
    base_w = links.pair(32)

    def copy_w(j):
        p = lax.rem(g + j, 32)
        return links.copy(base_w + j, grad_wide.at[p], grad_wide_in.at[g], 4 * p + m)

    for_range(1, 32, lambda j: copy_w(j).start())
    grad_normed = dot(grad_heads, weights_s[:, :576], ((1,), (1,)))
    part[1] = grad_normed.astype(BF).reshape(4, 128, 768)
    copies = reduce_start(1)
    grad_wide_in[g] = grad_wide[g]
    reduce_pass(1, copies)
    values = x[...].astype(F32)
    grad_input_o[...] = (
        grad_after_s[...] + rms_back(reduce_end(1, copies), values, rms_scale(values), gain_one)
    ).astype(BF)
    for_range(0, 8, lambda q: away(q, lambda k: copy_go(k).wait_send()))

    @pl.when(plane == m)
    def _():
        grad_out_in[g] = grad_out_s[place]

        def take(j):
            sender = lax.rem(g - j + 32, 32)
            pltpu.make_async_remote_copy(
                src_ref=grad_out_s.at[0],
                dst_ref=grad_out_in.at[sender],
                send_sem=send_sem.at[base_gs],
                recv_sem=recv_sem.at[base_gr + j],
                device_id=coords(4 * sender + m),
                device_id_type=MESH,
            ).wait_recv()

        for_range(1, 32, take)
        lay_b[...] = jnp.sum(grad_out_in[...].astype(F32), axis=0)

    for_range(1, 32, lambda j: copy_w(j).wait())
    lay_a[...] = jnp.sum(grad_wide_in[...].astype(F32), axis=0)

    for store in stores:
        store.wait()

    for k in range(4):
        fin[k, 0:6, 0:640] = lay_a[6 * k : 6 * k + 6]
        fin[k, 0:6, 640:1408] = lay_b[6 * k : 6 * k + 6]
    base_f = links.pair(4)

    def copy_f(j):
        k = lax.rem(m + j, 4)
        return links.copy(base_f + j, fin.at[k], fin_in.at[m], quad + k)

    for j in range(1, 4):
        copy_f(j).start()
    fin_in[m] = fin[m]
    for j in range(1, 4):
        copy_f(j).wait()
    grad_qkv = jnp.concatenate(
        [fin_in[k, 0:6, 192 * i : 192 * i + 192] for i in range(3) for k in range(4)], axis=1
    )
    grad_qkv_o[...] = grad_qkv
    by_row = jnp.sum(grad_qkv * qkv[...].astype(F32), axis=1, keepdims=True)
    by_row = by_row / columns_of[0:6, 0:1]
    grad_out_o[...] = fin_in[plane, 0:6, 640:1408]
    total = jnp.sum(fin_in[:, 0:6, 512:640], axis=0)
    total = jnp.where(iota((6, 128), 1) == 80, by_row, total)
    grad_small_o[...] = jnp.concatenate([total, jnp.zeros((2, 128), F32)], axis=0)


def results_kernel(
    result,
    grad_input,
    grad_qkv,
    grad_out,
    grad_small,
    grad_in,
    grad_eout,
    result_o,
    grad_input_o,
    grad_qkv_o,
    grad_out_o,
    grad_router_o,
    gain_one_o,
    gain_two_o,
    bias_o,
    grad_in_o,
    grad_eout_o,
    sems,
):
    whole = [
        (grad_in, grad_in_o),
        (grad_eout, grad_eout_o),
        (result, result_o),
        (grad_input, grad_input_o),
        (grad_qkv, grad_qkv_o),
        (grad_out, grad_out_o),
    ]
    copies = [
        pltpu.make_async_copy(source, target, sems.at[i])
        for i, (source, target) in enumerate(whole)
    ]
    for copy in copies:
        copy.start()
    values = grad_small[...]
    grad_router_o[...] = values[0:6, 64:80]
    lines = jnp.concatenate([values, jnp.zeros((120, 128), F32)], axis=0).T
    gain_one_o[...] = lines[80:81, 0:6]
    gain_two_o[...] = lines[81:82, 0:6]
    bias_o[...] = lines[82:83, 0:3]
    for copy in copies:
        copy.wait()


def choose_matrix():
    choose = np.zeros((DEPTH, EXPERTS * SLOT), np.float32)
    for kind in range(2):
        for source in range(EXPERTS):
            for slot in range(CAP):
                choose[
                    kind * HALF + source * CAP + slot, source * SLOT + kind * CAP + slot
                ] = 1.0
    return choose


def shape(*dims, dtype=BF):
    return jax.ShapeDtypeStruct(dims, dtype)


SCRATCH = [
    ((128, 768), BF),
    ((768, 384), BF),
    ((384, 768), BF),
    ((DEPTH, EXPERTS * SLOT), BF),
    ((128, 768), BF),
    ((768, 384), F32),
    ((384, 768), F32),
    ((1, 512), jnp.int32),
    ((8, 128), F32),
    ((4, 16, 640), BF),
    ((4, 16, 640), BF),
    ((16, 768), BF),
    ((4, 16, 768), BF),
    ((24, 640), F32),
    ((24, 768), F32),
    ((24, 640), BF),
    ((24, 768), BF),
    ((32, 24, 640), BF),
    ((768, 640), BF),
    ((8, 24, 768), BF),
    ((4, 128, 768), BF),
    ((512, 768), BF),
    ((512, 576), BF),
    ((6, 256, 256), F32),
    ((512, 192), BF),
    ((2, 4, 128, 768), BF),
    ((2, 128, 768), BF),
    ((2, 128, 768), BF),
    ((2, 128, 768), BF),
    ((2, 128, 768), BF),
    ((128, 768), F32),
    ((128, 768), BF),
    ((EXPERTS, SLOT, 768), BF),
    ((EXPERTS, SLOT, 768), BF),
    ((4, 2, DEPTH, 768), BF),
    ((4, 2, DEPTH, 768), BF),
    ((4, DEPTH, 768), BF),
    ((4, DEPTH, 768), BF),
    ((DEPTH, 768), BF),
    ((DEPTH, 768), BF),
    ((HALF, 768), BF),
    ((HALF, 768), BF),
    ((EXPERTS, SLOT, 768), BF),
    ((EXPERTS, SLOT, 768), BF),
    ((128, 768), F32),
    ((4, 128, 768), BF),
    ((32, 24, 640), BF),
    ((32, 24, 640), BF),
    ((8, 24, 768), BF),
    ((32, 24, 768), BF),
    ((4, 8, 1408), F32),
    ((4, 8, 1408), F32),
]
TRANSFERS = 256


def body(
    inputs,
    cotangent,
    routes,
    drop_mask,
    buckets,
    qkv_weight,
    out_weight,
    router_weight,
    attn_gain,
    ffn_gain,
    bias_table,
    expert_in,
    expert_out,
):
    vmem = pl.BlockSpec(memory_space=pltpu.VMEM)
    anywhere = pl.BlockSpec(memory_space=pl.ANY)
    outputs = pl.pallas_call(
        layer_kernel,
        out_shape=[
            shape(128, 768),
            shape(6, 2304, dtype=F32),
            shape(6, 768, dtype=F32),
            shape(8, 128, dtype=F32),
            shape(128, 768),
            shape(768, 384, dtype=F32),
            shape(384, 768, dtype=F32),
        ],
        in_specs=[vmem] * 10 + [anywhere] * 4,
        out_specs=[vmem] * 4 + [anywhere] * 3,
        scratch_shapes=[pltpu.VMEM(dims, dtype) for dims, dtype in SCRATCH]
        + [
            pltpu.SemaphoreType.DMA((TRANSFERS,)),
            pltpu.SemaphoreType.DMA((TRANSFERS,)),
            pltpu.SemaphoreType.DMA((7,)),
        ],
        compiler_params=pltpu.CompilerParams(
            collective_id=0, has_side_effects=True, vmem_limit_bytes=60 * 1024 * 1024
        ),
    )(
        inputs,
        routes.reshape(1, 128),
        drop_mask.reshape(1, 128),
        buckets.reshape(1, 511),
        qkv_weight,
        out_weight,
        router_weight,
        attn_gain.reshape(1, 6),
        ffn_gain.reshape(1, 6),
        bias_table.reshape(1, 3),
        cotangent,
        expert_in,
        expert_out,
        jnp.asarray(choose_matrix(), BF),
    )
    grad_input, grad_qkv, grad_out, grad_small, result, grad_in, grad_eout = outputs
    final = pl.pallas_call(
        results_kernel,
        out_shape=[
            shape(128, 768),
            shape(128, 768),
            shape(6, 2304, dtype=F32),
            shape(6, 768, dtype=F32),
            shape(6, 16, dtype=F32),
            shape(1, 6, dtype=F32),
            shape(1, 6, dtype=F32),
            shape(1, 3, dtype=F32),
            shape(768, 384, dtype=F32),
            shape(384, 768, dtype=F32),
        ],
        in_specs=[vmem] * 7,
        out_specs=[anywhere] * 4 + [vmem] * 4 + [anywhere] * 2,
        scratch_shapes=[pltpu.SemaphoreType.DMA((6,))],
        compiler_params=pltpu.CompilerParams(vmem_limit_bytes=60 * 1024 * 1024),
    )(result, grad_input, grad_qkv, grad_out, grad_small, grad_in, grad_eout)
    return (
        *final[:5],
        final[5].reshape(6),
        final[6].reshape(6),
        final[7].reshape(3),
        *final[8:],
    )


def solution(mesh):
    placed = (
        P(("fsdp", "sp"), None),
        P(("fsdp", "sp"), None),
        P(("fsdp", "sp"), None),
        P(("fsdp", "sp")),
        P(),
        P(("fsdp", "sp"), None),
        P(("fsdp", "sp"), None),
        P(("fsdp", "sp"), None),
        P(("fsdp", "sp")),
        P(("fsdp", "sp")),
        P(("fsdp", "sp")),
        P(None, ("fsdp", "sp")),
        P(("fsdp", "sp"), None),
    )
    return jax.shard_map(
        body,
        mesh=mesh,
        in_specs=placed,
        out_specs=(
            P(("fsdp", "sp"), None),
            P(("fsdp", "sp"), None),
            P(("fsdp", "sp"), None),
            P(("fsdp", "sp"), None),
            P(("fsdp", "sp"), None),
            P(("fsdp", "sp")),
            P(("fsdp", "sp")),
            P(("fsdp", "sp")),
            P(None, ("fsdp", "sp")),
            P(("fsdp", "sp"), None),
        ),
        check_vma=False,
    )
```

```python
import functools

import jax
import jax.numpy as jnp
import numpy as np
from jax import lax
from jax.experimental import pallas as pl
from jax.experimental.pallas import tpu as pltpu
from jax.sharding import PartitionSpec as P

HEADS = 12
HEAD_DIM = 64
EXPERTS = 16
BUCKETS = 32
CAP = 10
EPSILON = 1e-06
MESH = pl.DeviceIdType.MESH
BF = jnp.bfloat16
F32 = jnp.float32
SLOT = 24
GELU_C = 0.7978845608028654
GELU_A = 0.044715
DEPTH = 2 * EXPERTS * CAP
HALF = EXPERTS * CAP


def coords(flat):
    return (lax.div(flat, 2), lax.rem(flat, 2))


def for_range(low, high, fn):
    def step(j, carry):
        fn(j)
        return carry

    lax.fori_loop(low, high, step, 0)


def dot(a, b, dims=((1,), (0,)), precision=None):
    return lax.dot_general(
        a, b, (dims, ((), ())), precision=precision, preferred_element_type=F32
    )


def rms_scale(values):
    return lax.rsqrt(jnp.mean(values * values, axis=-1, keepdims=True) + EPSILON)


def rms_back(grad, values, scale, gain):
    weighted = grad * gain
    inner = jnp.mean(weighted * values, axis=-1, keepdims=True)
    return scale * weighted - values * (scale * scale * scale * inner)


def iota(shape, dim):
    return lax.broadcasted_iota(jnp.int32, shape, dim)


def ones_where(mask):
    return mask.astype(F32).astype(BF)


class Links:
    def __init__(self, send, recv):
        self.send, self.recv, self.used = send, recv, 0

    def pair(self, count=1):
        first = self.used
        self.used += count
        return first

    def copy(self, index, source, target, device):
        return pltpu.make_async_remote_copy(
            src_ref=source,
            dst_ref=target,
            send_sem=self.send.at[index],
            recv_sem=self.recv.at[index],
            device_id=coords(device),
            device_id_type=MESH,
        )


def rows_of(ref):
    blocks, rows, width = ref.shape
    return ref[...].astype(F32).reshape(blocks * rows, width).astype(BF)


def layer_kernel(
    x,
    routes,
    drop,
    buckets,
    qkv,
    out_w,
    router_w,
    gain_attn,
    gain_ffn,
    bias_w,
    cot_any,
    expert_in_any,
    expert_out_any,
    choose_any,
    grad_input_o,
    grad_qkv_o,
    grad_out_o,
    grad_small_o,
    result_any,
    grad_in_any,
    grad_eout_any,
    cot,
    expert_in,
    expert_out,
    choose,
    result_s,
    grad_in_o,
    grad_eout_o,
    offsets,
    lines_s,
    packs,
    packs_in,
    rawb,
    rawb_in,
    lay_a,
    lay_b,
    chunk_a,
    chunk_b,
    wide,
    weights_s,
    in_bucket,
    outs,
    tokens,
    normed_s,
    proj_s,
    probs_s,
    mixed_s,
    part,
    from_mate,
    merge,
    to_x,
    from_x,
    after_s,
    normed_two_s,
    send_s,
    arrived,
    rows_s,
    parts_s,
    mate_parts,
    sums_s,
    got_x,
    got_z,
    diag_x,
    diag_z,
    back_s,
    back_in,
    grad_after_s,
    grad_low,
    grad_wide,
    grad_wide_in,
    grad_out_s,
    grad_out_in,
    fin,
    fin_in,
    send_sem,
    recv_sem,
    local_sem,
):
    loads = [
        pltpu.make_async_copy(source, target, local_sem.at[i])
        for i, (source, target) in enumerate(
            [
                (cot_any, cot),
                (expert_in_any, expert_in),
                (expert_out_any, expert_out),
                (choose_any, choose),
            ]
        )
    ]
    stores = [
        pltpu.make_async_copy(source, target, local_sem.at[4 + i])
        for i, (source, target) in enumerate(
            [(result_s, result_any), (grad_in_o, grad_in_any), (grad_eout_o, grad_eout_any)]
        )
    ]
    links = Links(send_sem, recv_sem)
    fs, sp = lax.axis_index("fsdp"), lax.axis_index("sp")
    f = fs * 2 + sp
    m, g = lax.rem(f, 4), lax.div(f, 4)
    plane, place = lax.div(g, 8), lax.rem(g, 8)
    core, x_lo = lax.div(m, 2), lax.rem(m, 2)
    expert, member = lax.div(f, 8), lax.rem(f, 8)
    z_lo = lax.div(member, 4)
    x_hi, own_place = lax.rem(lax.div(expert, 2), 2), lax.div(expert, 4) * 2 + lax.rem(expert, 2)

    def side_of(k):
        return lax.rem(lax.rem(lax.div(k, 2), 2) + x_hi, 2)

    def place_in(k):
        return lax.div(k, 4) * 2 + lax.rem(k, 2)

    quad = f - m
    mate_m = (1 - core) * 2 + x_lo
    beside_m = core * 2 + (1 - x_lo)
    cross_m = (1 - core) * 2 + (1 - x_lo)
    mate, beside = quad + mate_m, quad + beside_m
    above = f - z_lo * 4 + (1 - z_lo) * 4
    spot = z_lo * 2 + x_lo
    spot_x = z_lo * 2 + (1 - x_lo)
    spot_z = (1 - z_lo) * 2 + x_lo
    spot_d = (1 - z_lo) * 2 + (1 - x_lo)

    barrier = pltpu.get_barrier_semaphore()

    def hello(device):
        pl.semaphore_signal(barrier, inc=1, device_id=coords(device), device_id_type=MESH)

    for j in range(1, 4):
        hello(quad + lax.rem(m + j, 4))
    for_range(1, 32, lambda j: hello(4 * lax.rem(g + j, 32) + m))

    for load in loads:
        load.start()
    tokens[m] = x[...]
    offsets[...] = jnp.full((1, 512), -1, jnp.int32)
    offsets[:, :511] = buckets[...]
    lines_s[...] = jnp.zeros((8, 128), F32)
    lines_s[0:1, 0:6] = gain_attn[...].astype(F32)
    lines_s[1:2, 0:6] = gain_ffn[...].astype(F32)
    lines_s[2:3, 0:3] = bias_w[...].astype(F32)
    lines_s[3:4] = routes[...].astype(F32)
    lines_s[4:5] = drop[...].astype(F32)
    columns_of = lines_s[...].T
    chosen = columns_of[:, 3:4].astype(jnp.int32)
    kept = columns_of[:, 4:5]
    weight = qkv[...].astype(F32)
    extra = jnp.concatenate(
        [router_w[...].astype(F32), columns_of[:6], jnp.zeros((6, 40), F32)], axis=1
    )
    for k in range(4):
        columns = [weight[:, 768 * i + 192 * k : 768 * i + 192 * k + 192] for i in range(3)]
        packs[k, 0:6] = jnp.concatenate(columns + [extra], axis=1).astype(BF)
    rawb[0:6] = out_w[...]
    pl.semaphore_wait(barrier, 34)

    base_p, base_b = links.pair(4), links.pair(4)

    def copy_pack(j):
        k = lax.rem(m + j, 4)
        return links.copy(base_p + j, packs.at[k], packs_in.at[m], quad + k)

    def copy_raw(j):
        return links.copy(base_b + j, rawb, rawb_in.at[m], quad + lax.rem(m + j, 4))

    for j in range(1, 4):
        copy_pack(j).start()
        copy_raw(j).start()
    packs_in[m] = packs[m]
    rawb_in[m] = rawb[...]

    def gather_four(buffer):
        first = links.pair(3)
        to_mate = links.copy(first, buffer.at[m], buffer.at[m], mate)
        to_beside = links.copy(first + 1, buffer.at[m], buffer.at[m], beside)
        passed = links.copy(first + 2, buffer.at[beside_m], buffer.at[beside_m], mate)
        return to_mate, to_beside, passed

    def finish_four(copies):
        to_mate, to_beside, passed = copies
        to_beside.wait_recv()
        passed.start()
        to_mate.wait()
        to_beside.wait_send()
        passed.wait()

    token_copies = gather_four(tokens)
    token_copies[1].start()
    token_copies[0].start()
    for j in range(1, 4):
        copy_pack(j).wait()
        copy_raw(j).wait()
    for k in range(4):
        lay_a[6 * k : 6 * k + 6] = packs_in[k].astype(F32)[0:6]
        lay_b[6 * k : 6 * k + 6] = rawb_in[k].astype(F32)[0:6]
    chunk_a[...] = lay_a[...].astype(BF)
    chunk_b[...] = lay_b[...].astype(BF)

    base_a = links.pair(32)
    base_o, base_r = links.pair(32), links.pair(8)

    def copy_a(j):
        return links.copy(base_a + j, chunk_a, wide.at[g], 4 * lax.rem(g + j, 32) + m)

    def copy_b(j, q):
        return pltpu.make_async_remote_copy(
            src_ref=chunk_b,
            dst_ref=outs.at[q],
            send_sem=send_sem.at[base_o + j],
            recv_sem=recv_sem.at[base_r + q],
            device_id=coords(4 * lax.rem(g + j, 32) + m),
            device_id_type=MESH,
        )

    for_range(1, 32, lambda j: copy_a(j).start())

    @pl.when(plane == m)
    def _():
        for_range(1, 32, lambda j: copy_b(j, place).start())
        outs[place] = chunk_b[...]

    wide[g] = chunk_a[...]
    finish_four(token_copies)
    values = tokens[...].astype(F32).reshape(512, 768)
    scaled = values * rms_scale(values)
    head_row = (iota((32, 24, 128), 1).reshape(768, 128) == 6 * m + iota((768, 128), 1)).astype(F32)
    head_row = jnp.where(iota((8, 768), 0) < 3, head_row.T[:8], 0.0)
    in_bucket[...] = ones_where(iota((32, 24, 512), 0).reshape(768, 512) == offsets[...])
    for_range(1, 32, lambda j: copy_a(j).wait())

    weights_s[...] = rows_of(wide)
    weights = weights_s[...]
    turned = weights[:, 512:640].astype(F32).T
    gain_one, gain_two, table = turned[80:81], turned[81:82], turned[82:83]
    router = weights[:, 576:592]
    by_offset = dot((head_row * table).astype(BF), in_bucket[...])
    normed = (scaled * gain_one).astype(BF)
    normed_s[...] = normed
    proj = dot(normed, weights[:, :576]).astype(BF)
    proj_s[...] = proj
    seqs = [[], []]
    for h in range(3):
        line = jnp.broadcast_to(by_offset[h : h + 1], (256, 512))
        bias = pltpu.roll(line, 257, 1, stride=1, stride_axis=0)[:, :256]
        for s in range(2):
            rows = slice(256 * s, 256 * s + 256)
            query = proj[rows, 64 * h : 64 * h + 64]
            key = proj[rows, 192 + 64 * h : 256 + 64 * h]
            value = proj[rows, 384 + 64 * h : 448 + 64 * h]
            scores = dot(query, key, ((1,), (1,))) + bias
            exponent = jnp.exp(scores - jnp.max(scores, axis=-1, keepdims=True))
            probs = exponent * (1.0 / jnp.sum(exponent, axis=-1, keepdims=True))
            probs_s[3 * s + h] = probs
            seqs[s].append(dot(probs.astype(BF), value).astype(BF))
    mixed = jnp.concatenate([jnp.concatenate(s, axis=1) for s in seqs], axis=0)
    mixed_s[...] = mixed

    def take_b(q):
        @pl.when(8 * m + q != g)
        def _():
            copy_b(1, q).wait_recv()

    for_range(0, 8, take_b)

    @pl.when(plane == m)
    def _():
        for_range(1, 32, lambda j: copy_b(j, place).wait_send())

    out_mine = rows_of(outs)
    part[0] = dot(mixed, out_mine).astype(BF).reshape(4, 128, 768)

    def reduce_start(n):
        first = links.pair(3)
        cross = links.copy(first, part.at[n, cross_m], merge.at[n], mate)
        straight = links.copy(first + 1, part.at[n, mate_m], from_mate.at[n], mate)
        over = links.copy(first + 2, to_x.at[n], from_x.at[n], beside)
        cross.start()
        straight.start()
        return cross, straight, over

    def reduce_pass(n, copies):
        cross, straight, over = copies
        cross.wait()
        to_x[n] = (part[n, beside_m].astype(F32) + merge[n].astype(F32)).astype(BF)
        over.start()

    def reduce_end(n, copies):
        cross, straight, over = copies
        straight.wait()
        over.wait()
        return part[n, m].astype(F32) + from_mate[n].astype(F32) + from_x[n].astype(F32)

    copies = reduce_start(0)
    reduce_pass(0, copies)
    hot = chosen == iota((128, EXPERTS), 1)
    earlier = iota((128, 128), 1) < iota((128, 128), 0)
    counts = dot(ones_where(earlier), ones_where(hot))
    slot = jnp.sum(jnp.where(hot, counts, 0.0), axis=-1, keepdims=True).astype(jnp.int32)
    target = jnp.where(kept > 0, chosen * SLOT + slot, -SLOT)
    lanes = iota((128, EXPERTS * SLOT), 1)
    pick_row, pick_grad = ones_where(lanes == target), ones_where(lanes == target + CAP)
    loads[0].wait()
    grad = cot[...].astype(F32)
    after = x[...].astype(F32) + reduce_end(0, copies)
    after_s[...] = after
    normed_two = (after * rms_scale(after) * gain_two).astype(BF)
    normed_two_s[...] = normed_two
    logits = dot(normed_two, router)
    exponent = jnp.exp(logits - jnp.max(logits, axis=-1, keepdims=True))
    router_probs = exponent / jnp.sum(exponent, axis=-1, keepdims=True)
    gates = jnp.sum(jnp.where(hot, router_probs, 0.0), axis=-1, keepdims=True)
    grad_y = (grad * (kept * gates)).astype(BF)
    slots = dot(
        jnp.concatenate([pick_row, pick_grad], axis=0),
        jnp.concatenate([normed_two, grad_y], axis=0),
        ((0,), (0,)),
    )
    send_s[...] = slots.astype(BF).reshape(EXPERTS, SLOT, 768)

    base_d, base_r = links.pair(EXPERTS), links.pair(EXPERTS)

    def group_at(side, i):
        return (lax.div(i, 2) * 2 + lax.rem(side + x_hi, 2)) * 2 + lax.rem(i, 2)

    def pair_copy(base, k, source, target):
        return pltpu.make_async_remote_copy(
            src_ref=source,
            dst_ref=target,
            send_sem=send_sem.at[base + k],
            recv_sem=recv_sem.at[base + expert],
            device_id=coords(8 * k + member),
            device_id_type=MESH,
        )

    def copy_d(k):
        return pair_copy(base_d, k, send_s.at[k], arrived.at[side_of(k), own_place])

    def arrival(side, i):
        k = group_at(side, i)
        return links.copy(base_d + k, send_s.at[k], arrived.at[side, i], 8 * k + member)

    def copy_r(k):
        return pair_copy(base_r, k, back_s.at[side_of(k), place_in(k)], back_in.at[expert])

    def come_back(k):
        return links.copy(base_r + k, back_s.at[0, 0], back_in.at[k], 8 * k + member)

    def next_group(j):
        return lax.rem(expert + j, EXPERTS)

    for_range(1, EXPERTS, lambda j: copy_d(next_group(j)).start())
    arrived[0, own_place] = send_s[expert]
    grad_in_o[...] = jnp.zeros_like(grad_in_o)
    grad_eout_o[...] = jnp.zeros_like(grad_eout_o)
    loads[3].wait()

    def take_rows(side):
        def take(i):
            if side == 0:
                pl.when(i != own_place)(lambda: arrival(side, i).wait_recv())
            else:
                arrival(side, i).wait_recv()

        for_range(0, 8, take)
        rows_s[spot, core, HALF * side : HALF * side + HALF] = dot(
            choose[...], rows_of(arrived.at[side])
        ).astype(BF)

    first_half, second_half = pl.ds(0, HALF), pl.ds(HALF, HALF)

    def rows_copy(place_of, half, device):
        ref = rows_s.at[place_of, core, half]
        return links.copy(links.pair(), ref, ref, device)

    out_x2 = rows_copy(spot, second_half, beside)
    out_z1 = rows_copy(spot, first_half, above)
    out_x1 = rows_copy(spot, first_half, beside)
    out_z2 = rows_copy(spot, second_half, above)
    out_m1 = rows_copy(spot, first_half, mate)
    out_m2 = rows_copy(spot, second_half, mate)
    pass_x = rows_copy(spot_z, first_half, beside)
    pass_z = rows_copy(spot_x, second_half, above)
    mate_x1, mate_x2 = (rows_copy(spot_x, h, mate) for h in (first_half, second_half))
    mate_z1, mate_z2 = (rows_copy(spot_z, h, mate) for h in (first_half, second_half))
    mate_d1, mate_d2 = (rows_copy(spot_d, h, mate) for h in (first_half, second_half))
    take_rows(0)
    for copy in (out_z1, out_x1, out_m1):
        copy.start()
    take_rows(1)
    for copy in (out_x2, out_z2, out_m2):
        copy.start()
    for_range(1, EXPERTS, lambda j: copy_d(next_group(j)).wait_send())

    def expert_step(place_of):
        both = rows_s[place_of]
        row = jnp.concatenate([both[:, :80], both[:, 160:240]], axis=1).reshape(DEPTH, 768)
        grad_row = jnp.concatenate([both[:, 80:160], both[:, 240:]], axis=1).reshape(DEPTH, 768)
        pre = dot(row, expert_in[...])
        square = pre * pre
        tanh = jnp.tanh(GELU_C * (pre + GELU_A * (pre * square)))
        half = 0.5 * (1.0 + tanh)
        act = (pre * half).astype(BF)
        slope = half + (0.5 * GELU_C) * pre * (1.0 - tanh * tanh) * (1.0 + 3.0 * GELU_A * square)
        out = dot(act, expert_out[...]).astype(BF).reshape(2, HALF, 768)
        parts_s[place_of, :, :80] = out[:, :80]
        parts_s[place_of, :, 160:240] = out[:, 80:]
        grad_act = dot(grad_row, expert_out[...], ((1,), (1,)))
        grad_pre = (grad_act * slope).astype(BF)
        out = dot(grad_pre, expert_in[...], ((1,), (1,))).astype(BF).reshape(2, HALF, 768)
        parts_s[place_of, :, 80:160] = out[:, :80]
        parts_s[place_of, :, 240:] = out[:, 80:]
        swap = links.copy(
            links.pair(), parts_s.at[place_of, 1 - core], mate_parts.at[place_of], mate
        )
        swap.start()
        grad_in_o[...] += dot(row, grad_pre, ((0,), (0,)))
        grad_eout_o[...] += dot(act, grad_row, ((0,), (0,)))
        swap.wait()
        sums_s[place_of] = (
            parts_s[place_of, core].astype(F32) + mate_parts[place_of].astype(F32)
        ).astype(BF)

    def sums_copy(place_of, half, target, device):
        copy = links.copy(links.pair(), sums_s.at[place_of, half], target, device)
        copy.start()
        return copy

    loads[1].wait()
    loads[2].wait()
    out_m1.wait()
    out_m2.wait()
    expert_step(spot)
    out_z1.wait()
    pass_x.start()
    mate_z1.start()
    out_x1.wait()
    mate_x1.start()
    out_x2.wait()
    pass_z.start()
    mate_x2.start()
    out_z2.wait()
    mate_z2.start()
    mate_x2.wait()
    mate_x1.wait()
    expert_step(spot_x)
    x_one = sums_copy(spot_x, first_half, got_x.at[first_half], beside)
    pass_z.wait()
    mate_d2.start()
    pass_x.wait()
    mate_d1.start()
    mate_z1.wait()
    mate_z2.wait()
    expert_step(spot_z)
    z_two = sums_copy(spot_z, second_half, got_z.at[second_half], above)
    mate_d1.wait()
    mate_d2.wait()
    expert_step(spot_d)
    d_one = sums_copy(spot_d, first_half, diag_x, beside)
    d_two = sums_copy(spot_d, second_half, diag_z, above)
    stores[1].start()
    stores[2].start()
    d_one.wait()
    sums_s[spot_z, :HALF] = (sums_s[spot_z, :HALF].astype(F32) + diag_x[...].astype(F32)).astype(
        BF
    )
    z_one = sums_copy(spot_z, first_half, got_z.at[first_half], above)
    d_two.wait()
    sums_s[spot_x, HALF:] = (sums_s[spot_x, HALF:].astype(F32) + diag_z[...].astype(F32)).astype(
        BF
    )
    x_two = sums_copy(spot_x, second_half, got_x.at[second_half], beside)
    for copy in (x_one, z_two, z_one, x_two):
        copy.wait()
    total = sums_s[spot].astype(F32) + got_x[...].astype(F32) + got_z[...].astype(F32)
    total = total.astype(BF)
    for side in range(2):
        slots = dot(choose[...], total[HALF * side : HALF * side + HALF], ((0,), (0,)))
        back_s[side] = slots.astype(BF).reshape(8, SLOT, 768)
    for_range(1, EXPERTS, lambda j: copy_r(next_group(j)).start())
    back_in[expert] = back_s[0, own_place]
    for_range(1, EXPERTS, lambda j: come_back(next_group(j)).wait_recv())
    for_range(1, EXPERTS, lambda j: copy_r(next_group(j)).wait_send())

    flat = rows_of(back_in)
    expert_y = dot(pick_row, flat)
    slot_grad = dot(pick_grad, flat)
    after = after_s[...]
    grad_gate = kept * jnp.sum(grad * expert_y, axis=-1, keepdims=True)
    grad_logits = ((grad_gate * gates) * (hot.astype(F32) - router_probs)).astype(BF)
    grad_normed = dot(grad_logits, router, ((1,), (1,))) + slot_grad
    scale = rms_scale(after)
    grad_after = grad + rms_back(grad_normed, after, scale, gain_two)
    grad_after_s[...] = grad_after
    grad_low[m] = grad_after.astype(BF)
    low_copies = gather_four(grad_low)
    low_copies[1].start()
    low_copies[0].start()
    result_s[...] = (after + (kept * gates) * expert_y).astype(BF)
    stores[0].start()
    grad_router = dot(grad_logits, normed_two_s[...], ((0,), (0,)))
    grad_gain_two = jnp.sum(grad_normed * after * scale, axis=0, keepdims=True)
    finish_four(low_copies)

    grad_proj = grad_low[...].reshape(512, 768)
    grad_mixed = dot(grad_proj, out_mine, ((1,), (1,))).astype(BF)
    grad_out = dot(mixed_s[...], grad_proj, ((0,), (0,)))
    grad_out_s[...] = grad_out.astype(BF).reshape(8, 24, 768)
    base_gs, base_gr = links.pair(8), links.pair(32)

    def copy_go(q):
        p = 8 * m + q
        return pltpu.make_async_remote_copy(
            src_ref=grad_out_s.at[q],
            dst_ref=grad_out_in.at[g],
            send_sem=send_sem.at[base_gs + q],
            recv_sem=recv_sem.at[base_gr + lax.rem(p - g + 32, 32)],
            device_id=coords(4 * p + m),
            device_id_type=MESH,
        )

    def away(q, fn):
        @pl.when(8 * m + q != g)
        def _():
            fn(q)

    for_range(0, 8, lambda q: away(q, lambda k: copy_go(k).start()))
    flip = ones_where(iota((256, 256), 0) + iota((256, 256), 1) == 255)
    pieces = [[[], [], []], [[], [], []]]
    sums = []
    for h in range(3):
        mirrored = jnp.zeros((256, 256), F32)
        for s in range(2):
            rows = slice(256 * s, 256 * s + 256)
            query = proj_s[rows, 64 * h : 64 * h + 64]
            key = proj_s[rows, 192 + 64 * h : 256 + 64 * h]
            value = proj_s[rows, 384 + 64 * h : 448 + 64 * h]
            grad_rows = grad_mixed[rows, 64 * h : 64 * h + 64]
            probs = probs_s[3 * s + h]
            grad_probs = dot(grad_rows, value, ((1,), (1,)))
            inner = jnp.sum(probs * grad_probs, axis=-1, keepdims=True)
            grad_scores = (probs * (grad_probs - inner)).astype(BF)
            mirrored = mirrored + dot(flip, grad_scores)
            pieces[s][0].append(dot(grad_scores, key).astype(BF))
            pieces[s][1].append(dot(grad_scores, query, ((0,), (0,))).astype(BF))
            pieces[s][2].append(dot(probs.astype(BF), grad_rows, ((0,), (0,))).astype(BF))
        line = jnp.concatenate([mirrored, jnp.zeros((256, 256), F32)], axis=1)
        line = pltpu.roll(line, 0, 1, stride=1, stride_axis=0)
        sums.append(jnp.sum(line, axis=0, keepdims=True))
    grad_heads = jnp.concatenate(
        [jnp.concatenate([p for part_of in s for p in part_of], axis=1) for s in pieces], axis=0
    )
    sums = jnp.concatenate(sums + [jnp.zeros((5, 512), F32)], axis=0)
    high = sums.astype(BF)
    rest = sums - high.astype(F32)
    middle = rest.astype(BF)
    low = (rest - middle.astype(F32)).astype(BF)
    grad_table = dot(
        jnp.concatenate([high.astype(F32), middle.astype(F32), low.astype(F32)], axis=0).astype(BF),
        in_bucket[...],
        ((1,), (1,)),
    )
    grad_table = (grad_table[16:24] + grad_table[8:16]) + grad_table[0:8]
    grad_table = jnp.sum(grad_table * head_row, axis=0, keepdims=True)
    lines = jnp.concatenate(
        [
            grad_router,
            jnp.zeros((1, 768), F32),
            grad_gain_two,
            grad_table,
            jnp.zeros((45, 768), F32),
        ],
        axis=0,
    )
    grad_qkv = dot(normed_s[...], grad_heads, ((0,), (0,)))
    grad_wide[...] = (
        jnp.concatenate([grad_qkv, lines.T], axis=1).reshape(32, 24, 640).astype(BF)
    )
    base_w = links.pair(32)

    def copy_w(j):
        p = lax.rem(g + j, 32)
        return links.copy(base_w + j, grad_wide.at[p], grad_wide_in.at[g], 4 * p + m)

    for_range(1, 32, lambda j: copy_w(j).start())
    grad_normed = dot(grad_heads, weights_s[:, :576], ((1,), (1,)))
    part[1] = grad_normed.astype(BF).reshape(4, 128, 768)
    copies = reduce_start(1)
    grad_wide_in[g] = grad_wide[g]
    reduce_pass(1, copies)
    values = x[...].astype(F32)
    grad_input_o[...] = (
        grad_after_s[...] + rms_back(reduce_end(1, copies), values, rms_scale(values), gain_one)
    ).astype(BF)
    for_range(0, 8, lambda q: away(q, lambda k: copy_go(k).wait_send()))

    @pl.when(plane == m)
    def _():
        grad_out_in[g] = grad_out_s[place]

        def take(j):
            sender = lax.rem(g - j + 32, 32)
            pltpu.make_async_remote_copy(
                src_ref=grad_out_s.at[0],
                dst_ref=grad_out_in.at[sender],
                send_sem=send_sem.at[base_gs],
                recv_sem=recv_sem.at[base_gr + j],
                device_id=coords(4 * sender + m),
                device_id_type=MESH,
            ).wait_recv()

        for_range(1, 32, take)
        lay_b[...] = jnp.sum(grad_out_in[...].astype(F32), axis=0)

    for_range(1, 32, lambda j: copy_w(j).wait())
    lay_a[...] = jnp.sum(grad_wide_in[...].astype(F32), axis=0)

    for store in stores:
        store.wait()

    for k in range(4):
        fin[k, 0:6, 0:640] = lay_a[6 * k : 6 * k + 6]
        fin[k, 0:6, 640:1408] = lay_b[6 * k : 6 * k + 6]
    base_f = links.pair(4)

    def copy_f(j):
        k = lax.rem(m + j, 4)
        return links.copy(base_f + j, fin.at[k], fin_in.at[m], quad + k)

    for j in range(1, 4):
        copy_f(j).start()
    fin_in[m] = fin[m]
    for j in range(1, 4):
        copy_f(j).wait()
    grad_qkv = jnp.concatenate(
        [fin_in[k, 0:6, 192 * i : 192 * i + 192] for i in range(3) for k in range(4)], axis=1
    )
    grad_qkv_o[...] = grad_qkv
    by_row = jnp.sum(grad_qkv * qkv[...].astype(F32), axis=1, keepdims=True)
    by_row = by_row / columns_of[0:6, 0:1]
    grad_out_o[...] = fin_in[plane, 0:6, 640:1408]
    total = jnp.sum(fin_in[:, 0:6, 512:640], axis=0)
    total = jnp.where(iota((6, 128), 1) == 80, by_row, total)
    grad_small_o[...] = jnp.concatenate([total, jnp.zeros((2, 128), F32)], axis=0)


def results_kernel(
    result,
    grad_input,
    grad_qkv,
    grad_out,
    grad_small,
    grad_in,
    grad_eout,
    result_o,
    grad_input_o,
    grad_qkv_o,
    grad_out_o,
    grad_router_o,
    gain_one_o,
    gain_two_o,
    bias_o,
    grad_in_o,
    grad_eout_o,
    sems,
):
    whole = [
        (grad_in, grad_in_o),
        (grad_eout, grad_eout_o),
        (result, result_o),
        (grad_input, grad_input_o),
        (grad_qkv, grad_qkv_o),
        (grad_out, grad_out_o),
    ]
    copies = [
        pltpu.make_async_copy(source, target, sems.at[i])
        for i, (source, target) in enumerate(whole)
    ]
    for copy in copies:
        copy.start()
    values = grad_small[...]
    grad_router_o[...] = values[0:6, 64:80]
    lines = jnp.concatenate([values, jnp.zeros((120, 128), F32)], axis=0).T
    gain_one_o[...] = lines[80:81, 0:6]
    gain_two_o[...] = lines[81:82, 0:6]
    bias_o[...] = lines[82:83, 0:3]
    for copy in copies:
        copy.wait()


def choose_matrix():
    choose = np.zeros((HALF, 8 * SLOT), np.float32)
    for kind in range(2):
        for source in range(8):
            for slot in range(CAP):
                choose[kind * 80 + source * CAP + slot, source * SLOT + kind * CAP + slot] = 1.0
    return choose


def shape(*dims, dtype=BF):
    return jax.ShapeDtypeStruct(dims, dtype)


SCRATCH = [
    ((128, 768), BF),
    ((768, 384), BF),
    ((384, 768), BF),
    ((HALF, 8 * SLOT), BF),
    ((128, 768), BF),
    ((768, 384), F32),
    ((384, 768), F32),
    ((1, 512), jnp.int32),
    ((8, 128), F32),
    ((4, 16, 640), BF),
    ((4, 16, 640), BF),
    ((16, 768), BF),
    ((4, 16, 768), BF),
    ((24, 640), F32),
    ((24, 768), F32),
    ((24, 640), BF),
    ((24, 768), BF),
    ((32, 24, 640), BF),
    ((768, 640), BF),
    ((768, 512), BF),
    ((8, 24, 768), BF),
    ((4, 128, 768), BF),
    ((512, 768), BF),
    ((512, 576), BF),
    ((6, 256, 256), F32),
    ((512, 192), BF),
    ((2, 4, 128, 768), BF),
    ((2, 128, 768), BF),
    ((2, 128, 768), BF),
    ((2, 128, 768), BF),
    ((2, 128, 768), BF),
    ((128, 768), F32),
    ((128, 768), BF),
    ((EXPERTS, SLOT, 768), BF),
    ((2, 8, SLOT, 768), BF),
    ((4, 2, DEPTH, 768), BF),
    ((4, 2, DEPTH, 768), BF),
    ((4, DEPTH, 768), BF),
    ((4, DEPTH, 768), BF),
    ((DEPTH, 768), BF),
    ((DEPTH, 768), BF),
    ((HALF, 768), BF),
    ((HALF, 768), BF),
    ((2, 8, SLOT, 768), BF),
    ((EXPERTS, SLOT, 768), BF),
    ((128, 768), F32),
    ((4, 128, 768), BF),
    ((32, 24, 640), BF),
    ((32, 24, 640), BF),
    ((8, 24, 768), BF),
    ((32, 24, 768), BF),
    ((4, 8, 1408), F32),
    ((4, 8, 1408), F32),
]
TRANSFERS = 256


def body(
    inputs,
    cotangent,
    routes,
    drop_mask,
    buckets,
    qkv_weight,
    out_weight,
    router_weight,
    attn_gain,
    ffn_gain,
    bias_table,
    expert_in,
    expert_out,
):
    vmem = pl.BlockSpec(memory_space=pltpu.VMEM)
    anywhere = pl.BlockSpec(memory_space=pl.ANY)
    outputs = pl.pallas_call(
        layer_kernel,
        out_shape=[
            shape(128, 768),
            shape(6, 2304, dtype=F32),
            shape(6, 768, dtype=F32),
            shape(8, 128, dtype=F32),
            shape(128, 768),
            shape(768, 384, dtype=F32),
            shape(384, 768, dtype=F32),
        ],
        in_specs=[vmem] * 10 + [anywhere] * 4,
        out_specs=[vmem] * 4 + [anywhere] * 3,
        scratch_shapes=[pltpu.VMEM(dims, dtype) for dims, dtype in SCRATCH]
        + [
            pltpu.SemaphoreType.DMA((TRANSFERS,)),
            pltpu.SemaphoreType.DMA((TRANSFERS,)),
            pltpu.SemaphoreType.DMA((7,)),
        ],
        compiler_params=pltpu.CompilerParams(
            collective_id=0, has_side_effects=True, vmem_limit_bytes=60 * 1024 * 1024
        ),
    )(
        inputs,
        routes.reshape(1, 128),
        drop_mask.reshape(1, 128),
        buckets.reshape(1, 511),
        qkv_weight,
        out_weight,
        router_weight,
        attn_gain.reshape(1, 6),
        ffn_gain.reshape(1, 6),
        bias_table.reshape(1, 3),
        cotangent,
        expert_in,
        expert_out,
        jnp.asarray(choose_matrix(), BF),
    )
    grad_input, grad_qkv, grad_out, grad_small, result, grad_in, grad_eout = outputs
    final = pl.pallas_call(
        results_kernel,
        out_shape=[
            shape(128, 768),
            shape(128, 768),
            shape(6, 2304, dtype=F32),
            shape(6, 768, dtype=F32),
            shape(6, 16, dtype=F32),
            shape(1, 6, dtype=F32),
            shape(1, 6, dtype=F32),
            shape(1, 3, dtype=F32),
            shape(768, 384, dtype=F32),
            shape(384, 768, dtype=F32),
        ],
        in_specs=[vmem] * 7,
        out_specs=[anywhere] * 4 + [vmem] * 4 + [anywhere] * 2,
        scratch_shapes=[pltpu.SemaphoreType.DMA((6,))],
        compiler_params=pltpu.CompilerParams(vmem_limit_bytes=60 * 1024 * 1024),
    )(result, grad_input, grad_qkv, grad_out, grad_small, grad_in, grad_eout)
    return (
        *final[:5],
        final[5].reshape(6),
        final[6].reshape(6),
        final[7].reshape(3),
        *final[8:],
    )


def solution(mesh):
    placed = (
        P(("fsdp", "sp"), None),
        P(("fsdp", "sp"), None),
        P(("fsdp", "sp"), None),
        P(("fsdp", "sp")),
        P(),
        P(("fsdp", "sp"), None),
        P(("fsdp", "sp"), None),
        P(("fsdp", "sp"), None),
        P(("fsdp", "sp")),
        P(("fsdp", "sp")),
        P(("fsdp", "sp")),
        P(None, ("fsdp", "sp")),
        P(("fsdp", "sp"), None),
    )
    return jax.shard_map(
        body,
        mesh=mesh,
        in_specs=placed,
        out_specs=(
            P(("fsdp", "sp"), None),
            P(("fsdp", "sp"), None),
            P(("fsdp", "sp"), None),
            P(("fsdp", "sp"), None),
            P(("fsdp", "sp"), None),
            P(("fsdp", "sp")),
            P(("fsdp", "sp")),
            P(("fsdp", "sp")),
            P(None, ("fsdp", "sp")),
            P(("fsdp", "sp"), None),
        ),
        check_vma=False,
    )
```

```python
import functools

import jax
import jax.numpy as jnp
import numpy as np
from jax import lax
from jax.experimental import pallas as pl
from jax.experimental.pallas import tpu as pltpu
from jax.sharding import PartitionSpec as P

HEADS = 12
HEAD_DIM = 64
EXPERTS = 16
BUCKETS = 32
CAP = 10
EPSILON = 1e-06
MESH = pl.DeviceIdType.MESH
BF = jnp.bfloat16
F32 = jnp.float32
SLOT = 24
GELU_C = 0.7978845608028654
GELU_A = 0.044715
DEPTH = 2 * EXPERTS * CAP
HALF = EXPERTS * CAP


def coords(flat):
    return (lax.div(flat, 2), lax.rem(flat, 2))


def for_range(low, high, fn):
    def step(j, carry):
        fn(j)
        return carry

    lax.fori_loop(low, high, step, 0)


def dot(a, b, dims=((1,), (0,)), precision=None):
    return lax.dot_general(
        a, b, (dims, ((), ())), precision=precision, preferred_element_type=F32
    )


def rms_scale(values):
    return lax.rsqrt(jnp.mean(values * values, axis=-1, keepdims=True) + EPSILON)


def rms_back(grad, values, scale, gain):
    weighted = grad * gain
    inner = jnp.mean(weighted * values, axis=-1, keepdims=True)
    return scale * weighted - values * (scale * scale * scale * inner)


def iota(shape, dim):
    return lax.broadcasted_iota(jnp.int32, shape, dim)


def ones_where(mask):
    return mask.astype(F32).astype(BF)


class Links:
    def __init__(self, send, recv):
        self.send, self.recv, self.used = send, recv, 0

    def pair(self, count=1):
        first = self.used
        self.used += count
        return first

    def copy(self, index, source, target, device):
        return pltpu.make_async_remote_copy(
            src_ref=source,
            dst_ref=target,
            send_sem=self.send.at[index],
            recv_sem=self.recv.at[index],
            device_id=coords(device),
            device_id_type=MESH,
        )


def rows_of(ref):
    blocks, rows, width = ref.shape
    return ref[...].astype(F32).reshape(blocks * rows, width).astype(BF)


def layer_kernel(
    x_any,
    routes_any,
    drop_any,
    buckets_any,
    qkv_any,
    out_w_any,
    router_w_any,
    gain_attn_any,
    gain_ffn_any,
    bias_w_any,
    cot_any,
    expert_in_any,
    expert_out_any,
    choose_any,
    grad_input_o,
    grad_qkv_o,
    grad_out_o,
    grad_small_o,
    result_any,
    grad_in_any,
    grad_eout_any,
    x,
    routes,
    drop,
    buckets,
    qkv,
    out_w,
    router_w,
    gain_attn,
    gain_ffn,
    bias_w,
    cot,
    expert_in,
    expert_out,
    choose,
    result_s,
    grad_in_o,
    grad_eout_o,
    offsets,
    lines_s,
    packs,
    packs_in,
    rawb,
    rawb_in,
    lay_a,
    lay_b,
    chunk_a,
    chunk_b,
    wide,
    weights_s,
    in_bucket,
    outs,
    tokens,
    normed_s,
    proj_s,
    probs_s,
    mixed_s,
    part,
    from_mate,
    merge,
    to_x,
    from_x,
    after_s,
    normed_two_s,
    send_s,
    arrived,
    rows_s,
    parts_s,
    mate_parts,
    sums_s,
    got_x,
    got_z,
    diag_x,
    diag_z,
    back_s,
    back_in,
    grad_after_s,
    grad_low,
    grad_wide,
    grad_wide_in,
    grad_out_s,
    grad_out_in,
    fin,
    fin_in,
    send_sem,
    recv_sem,
    local_sem,
):
    loads = [
        pltpu.make_async_copy(source, target, local_sem.at[i])
        for i, (source, target) in enumerate(
            [
                (cot_any, cot),
                (expert_in_any, expert_in),
                (expert_out_any, expert_out),
                (choose_any, choose),
            ]
        )
    ]
    early = [
        pltpu.make_async_copy(source, target, local_sem.at[7 + i])
        for i, (source, target) in enumerate(
            [
                (x_any, x),
                (routes_any, routes),
                (drop_any, drop),
                (buckets_any, buckets),
                (qkv_any, qkv),
                (out_w_any, out_w),
                (router_w_any, router_w),
                (gain_attn_any, gain_attn),
                (gain_ffn_any, gain_ffn),
                (bias_w_any, bias_w),
            ]
        )
    ]
    stores = [
        pltpu.make_async_copy(source, target, local_sem.at[4 + i])
        for i, (source, target) in enumerate(
            [(result_s, result_any), (grad_in_o, grad_in_any), (grad_eout_o, grad_eout_any)]
        )
    ]
    links = Links(send_sem, recv_sem)
    fs, sp = lax.axis_index("fsdp"), lax.axis_index("sp")
    f = fs * 2 + sp
    m, g = lax.rem(f, 4), lax.div(f, 4)
    plane, place = lax.div(g, 8), lax.rem(g, 8)
    core, x_lo = lax.div(m, 2), lax.rem(m, 2)
    expert, member = lax.div(f, 8), lax.rem(f, 8)
    z_lo = lax.div(member, 4)
    x_hi, own_place = lax.rem(lax.div(expert, 2), 2), lax.div(expert, 4) * 2 + lax.rem(expert, 2)

    def side_of(k):
        return lax.rem(lax.rem(lax.div(k, 2), 2) + x_hi, 2)

    def place_in(k):
        return lax.div(k, 4) * 2 + lax.rem(k, 2)

    quad = f - m
    mate_m = (1 - core) * 2 + x_lo
    beside_m = core * 2 + (1 - x_lo)
    cross_m = (1 - core) * 2 + (1 - x_lo)
    mate, beside = quad + mate_m, quad + beside_m
    above = f - z_lo * 4 + (1 - z_lo) * 4
    spot = z_lo * 2 + x_lo
    spot_x = z_lo * 2 + (1 - x_lo)
    spot_z = (1 - z_lo) * 2 + x_lo
    spot_d = (1 - z_lo) * 2 + (1 - x_lo)

    barrier = pltpu.get_barrier_semaphore()

    def hello(device):
        pl.semaphore_signal(barrier, inc=1, device_id=coords(device), device_id_type=MESH)

    for j in range(1, 4):
        hello(quad + lax.rem(m + j, 4))
    for_range(1, 32, lambda j: hello(4 * lax.rem(g + j, 32) + m))

    for load in early:
        load.start()
    for load in loads:
        load.start()
    for load in early:
        load.wait()
    tokens[m] = x[...]
    offsets[...] = jnp.full((1, 512), -1, jnp.int32)
    offsets[:, :511] = buckets[...]
    lines_s[...] = jnp.zeros((8, 128), F32)
    lines_s[0:1, 0:6] = gain_attn[...].astype(F32)
    lines_s[1:2, 0:6] = gain_ffn[...].astype(F32)
    lines_s[2:3, 0:3] = bias_w[...].astype(F32)
    lines_s[3:4] = routes[...].astype(F32)
    lines_s[4:5] = drop[...].astype(F32)
    columns_of = lines_s[...].T
    chosen = columns_of[:, 3:4].astype(jnp.int32)
    kept = columns_of[:, 4:5]
    weight = qkv[...].astype(F32)
    extra = jnp.concatenate(
        [router_w[...].astype(F32), columns_of[:6], jnp.zeros((6, 40), F32)], axis=1
    )
    for k in range(4):
        columns = [weight[:, 768 * i + 192 * k : 768 * i + 192 * k + 192] for i in range(3)]
        packs[k, 0:6] = jnp.concatenate(columns + [extra], axis=1).astype(BF)
    rawb[0:6] = out_w[...]
    pl.semaphore_wait(barrier, 34)

    base_p, base_b = links.pair(4), links.pair(4)

    def copy_pack(j):
        k = lax.rem(m + j, 4)
        return links.copy(base_p + j, packs.at[k], packs_in.at[m], quad + k)

    def copy_raw(j):
        return links.copy(base_b + j, rawb, rawb_in.at[m], quad + lax.rem(m + j, 4))

    for j in range(1, 4):
        copy_pack(j).start()
        copy_raw(j).start()
    packs_in[m] = packs[m]
    rawb_in[m] = rawb[...]

    def gather_four(buffer):
        first = links.pair(3)
        to_mate = links.copy(first, buffer.at[m], buffer.at[m], mate)
        to_beside = links.copy(first + 1, buffer.at[m], buffer.at[m], beside)
        passed = links.copy(first + 2, buffer.at[beside_m], buffer.at[beside_m], mate)
        return to_mate, to_beside, passed

    def finish_four(copies):
        to_mate, to_beside, passed = copies
        to_beside.wait_recv()
        passed.start()
        to_mate.wait()
        to_beside.wait_send()
        passed.wait()

    token_copies = gather_four(tokens)
    token_copies[1].start()
    token_copies[0].start()
    for j in range(1, 4):
        copy_pack(j).wait()
        copy_raw(j).wait()
    for k in range(4):
        lay_a[6 * k : 6 * k + 6] = packs_in[k].astype(F32)[0:6]
        lay_b[6 * k : 6 * k + 6] = rawb_in[k].astype(F32)[0:6]
    chunk_a[...] = lay_a[...].astype(BF)
    chunk_b[...] = lay_b[...].astype(BF)

    base_a = links.pair(32)
    base_o, base_r = links.pair(32), links.pair(8)

    def copy_a(j):
        return links.copy(base_a + j, chunk_a, wide.at[g], 4 * lax.rem(g + j, 32) + m)

    def copy_b(j, q):
        return pltpu.make_async_remote_copy(
            src_ref=chunk_b,
            dst_ref=outs.at[q],
            send_sem=send_sem.at[base_o + j],
            recv_sem=recv_sem.at[base_r + q],
            device_id=coords(4 * lax.rem(g + j, 32) + m),
            device_id_type=MESH,
        )

    for_range(1, 32, lambda j: copy_a(j).start())

    @pl.when(plane == m)
    def _():
        for_range(1, 32, lambda j: copy_b(j, place).start())
        outs[place] = chunk_b[...]

    wide[g] = chunk_a[...]
    finish_four(token_copies)
    values = tokens[...].astype(F32).reshape(512, 768)
    scaled = values * rms_scale(values)
    head_row = (iota((32, 24, 128), 1).reshape(768, 128) == 6 * m + iota((768, 128), 1)).astype(F32)
    head_row = jnp.where(iota((8, 768), 0) < 3, head_row.T[:8], 0.0)
    in_bucket[...] = ones_where(iota((32, 24, 512), 0).reshape(768, 512) == offsets[...])
    for_range(1, 32, lambda j: copy_a(j).wait())

    weights_s[...] = rows_of(wide)
    weights = weights_s[...]
    turned = weights[:, 512:640].astype(F32).T
    gain_one, gain_two, table = turned[80:81], turned[81:82], turned[82:83]
    router = weights[:, 576:592]
    by_offset = dot((head_row * table).astype(BF), in_bucket[...])
    normed = (scaled * gain_one).astype(BF)
    normed_s[...] = normed
    proj = dot(normed, weights[:, :576]).astype(BF)
    proj_s[...] = proj
    seqs = [[], []]
    for h in range(3):
        line = jnp.broadcast_to(by_offset[h : h + 1], (256, 512))
        bias = pltpu.roll(line, 257, 1, stride=1, stride_axis=0)[:, :256]
        for s in range(2):
            rows = slice(256 * s, 256 * s + 256)
            query = proj[rows, 64 * h : 64 * h + 64]
            key = proj[rows, 192 + 64 * h : 256 + 64 * h]
            value = proj[rows, 384 + 64 * h : 448 + 64 * h]
            scores = dot(query, key, ((1,), (1,))) + bias
            exponent = jnp.exp(scores - jnp.max(scores, axis=-1, keepdims=True))
            probs = exponent * (1.0 / jnp.sum(exponent, axis=-1, keepdims=True))
            probs_s[3 * s + h] = probs
            seqs[s].append(dot(probs.astype(BF), value).astype(BF))
    mixed = jnp.concatenate([jnp.concatenate(s, axis=1) for s in seqs], axis=0)
    mixed_s[...] = mixed

    def take_b(q):
        @pl.when(8 * m + q != g)
        def _():
            copy_b(1, q).wait_recv()

    for_range(0, 8, take_b)

    @pl.when(plane == m)
    def _():
        for_range(1, 32, lambda j: copy_b(j, place).wait_send())

    out_mine = rows_of(outs)
    part[0] = dot(mixed, out_mine).astype(BF).reshape(4, 128, 768)

    def reduce_start(n):
        first = links.pair(3)
        cross = links.copy(first, part.at[n, cross_m], merge.at[n], mate)
        straight = links.copy(first + 1, part.at[n, mate_m], from_mate.at[n], mate)
        over = links.copy(first + 2, to_x.at[n], from_x.at[n], beside)
        cross.start()
        straight.start()
        return cross, straight, over

    def reduce_pass(n, copies):
        cross, straight, over = copies
        cross.wait()
        to_x[n] = (part[n, beside_m].astype(F32) + merge[n].astype(F32)).astype(BF)
        over.start()

    def reduce_end(n, copies):
        cross, straight, over = copies
        straight.wait()
        over.wait()
        return part[n, m].astype(F32) + from_mate[n].astype(F32) + from_x[n].astype(F32)

    copies = reduce_start(0)
    reduce_pass(0, copies)
    hot = chosen == iota((128, EXPERTS), 1)
    earlier = iota((128, 128), 1) < iota((128, 128), 0)
    counts = dot(ones_where(earlier), ones_where(hot))
    slot = jnp.sum(jnp.where(hot, counts, 0.0), axis=-1, keepdims=True).astype(jnp.int32)
    target = jnp.where(kept > 0, chosen * SLOT + slot, -SLOT)
    lanes = iota((128, EXPERTS * SLOT), 1)
    pick_row, pick_grad = ones_where(lanes == target), ones_where(lanes == target + CAP)
    loads[0].wait()
    grad = cot[...].astype(F32)
    after = x[...].astype(F32) + reduce_end(0, copies)
    after_s[...] = after
    normed_two = (after * rms_scale(after) * gain_two).astype(BF)
    normed_two_s[...] = normed_two
    logits = dot(normed_two, router)
    exponent = jnp.exp(logits - jnp.max(logits, axis=-1, keepdims=True))
    router_probs = exponent / jnp.sum(exponent, axis=-1, keepdims=True)
    gates = jnp.sum(jnp.where(hot, router_probs, 0.0), axis=-1, keepdims=True)
    grad_y = (grad * (kept * gates)).astype(BF)
    slots = dot(
        jnp.concatenate([pick_row, pick_grad], axis=0),
        jnp.concatenate([normed_two, grad_y], axis=0),
        ((0,), (0,)),
    )
    send_s[...] = slots.astype(BF).reshape(EXPERTS, SLOT, 768)

    base_d, base_r = links.pair(EXPERTS), links.pair(EXPERTS)

    def group_at(side, i):
        return (lax.div(i, 2) * 2 + lax.rem(side + x_hi, 2)) * 2 + lax.rem(i, 2)

    def pair_copy(base, k, source, target):
        return pltpu.make_async_remote_copy(
            src_ref=source,
            dst_ref=target,
            send_sem=send_sem.at[base + k],
            recv_sem=recv_sem.at[base + expert],
            device_id=coords(8 * k + member),
            device_id_type=MESH,
        )

    def copy_d(k):
        return pair_copy(base_d, k, send_s.at[k], arrived.at[side_of(k), own_place])

    def arrival(side, i):
        k = group_at(side, i)
        return links.copy(base_d + k, send_s.at[k], arrived.at[side, i], 8 * k + member)

    def copy_r(k):
        return pair_copy(base_r, k, back_s.at[side_of(k), place_in(k)], back_in.at[expert])

    def come_back(k):
        return links.copy(base_r + k, back_s.at[0, 0], back_in.at[k], 8 * k + member)

    def next_group(j):
        return lax.rem(expert + j, EXPERTS)

    for_range(1, EXPERTS, lambda j: copy_d(next_group(j)).start())
    arrived[0, own_place] = send_s[expert]
    grad_in_o[...] = jnp.zeros_like(grad_in_o)
    grad_eout_o[...] = jnp.zeros_like(grad_eout_o)
    loads[3].wait()

    def take_rows(side):
        def take(i):
            if side == 0:
                pl.when(i != own_place)(lambda: arrival(side, i).wait_recv())
            else:
                arrival(side, i).wait_recv()

        for_range(0, 8, take)
        rows_s[spot, core, HALF * side : HALF * side + HALF] = dot(
            choose[...], rows_of(arrived.at[side])
        ).astype(BF)

    first_half, second_half = pl.ds(0, HALF), pl.ds(HALF, HALF)

    def rows_copy(place_of, half, device):
        ref = rows_s.at[place_of, core, half]
        return links.copy(links.pair(), ref, ref, device)

    out_x2 = rows_copy(spot, second_half, beside)
    out_z1 = rows_copy(spot, first_half, above)
    out_x1 = rows_copy(spot, first_half, beside)
    out_z2 = rows_copy(spot, second_half, above)
    out_m1 = rows_copy(spot, first_half, mate)
    out_m2 = rows_copy(spot, second_half, mate)
    pass_x = rows_copy(spot_z, first_half, beside)
    pass_z = rows_copy(spot_x, second_half, above)
    mate_x1, mate_x2 = (rows_copy(spot_x, h, mate) for h in (first_half, second_half))
    mate_z1, mate_z2 = (rows_copy(spot_z, h, mate) for h in (first_half, second_half))
    mate_d1, mate_d2 = (rows_copy(spot_d, h, mate) for h in (first_half, second_half))
    take_rows(0)
    for copy in (out_z1, out_x1, out_m1):
        copy.start()
    take_rows(1)
    for copy in (out_x2, out_z2, out_m2):
        copy.start()
    for_range(1, EXPERTS, lambda j: copy_d(next_group(j)).wait_send())

    def expert_step(place_of):
        both = rows_s[place_of]
        row = jnp.concatenate([both[:, :80], both[:, 160:240]], axis=1).reshape(DEPTH, 768)
        grad_row = jnp.concatenate([both[:, 80:160], both[:, 240:]], axis=1).reshape(DEPTH, 768)
        pre = dot(row, expert_in[...])
        square = pre * pre
        tanh = jnp.tanh(GELU_C * (pre + GELU_A * (pre * square)))
        half = 0.5 * (1.0 + tanh)
        act = (pre * half).astype(BF)
        slope = half + (0.5 * GELU_C) * pre * (1.0 - tanh * tanh) * (1.0 + 3.0 * GELU_A * square)
        out = dot(act, expert_out[...]).astype(BF).reshape(2, HALF, 768)
        parts_s[place_of, :, :80] = out[:, :80]
        parts_s[place_of, :, 160:240] = out[:, 80:]
        grad_act = dot(grad_row, expert_out[...], ((1,), (1,)))
        grad_pre = (grad_act * slope).astype(BF)
        out = dot(grad_pre, expert_in[...], ((1,), (1,))).astype(BF).reshape(2, HALF, 768)
        parts_s[place_of, :, 80:160] = out[:, :80]
        parts_s[place_of, :, 240:] = out[:, 80:]
        swap = links.copy(
            links.pair(), parts_s.at[place_of, 1 - core], mate_parts.at[place_of], mate
        )
        swap.start()
        grad_in_o[...] += dot(row, grad_pre, ((0,), (0,)))
        grad_eout_o[...] += dot(act, grad_row, ((0,), (0,)))
        swap.wait()
        sums_s[place_of] = (
            parts_s[place_of, core].astype(F32) + mate_parts[place_of].astype(F32)
        ).astype(BF)

    def sums_copy(place_of, half, target, device):
        copy = links.copy(links.pair(), sums_s.at[place_of, half], target, device)
        copy.start()
        return copy

    loads[1].wait()
    loads[2].wait()
    out_m1.wait()
    out_m2.wait()
    expert_step(spot)
    out_z1.wait()
    pass_x.start()
    mate_z1.start()
    out_x1.wait()
    mate_x1.start()
    out_x2.wait()
    pass_z.start()
    mate_x2.start()
    out_z2.wait()
    mate_z2.start()
    mate_x2.wait()
    mate_x1.wait()
    expert_step(spot_x)
    x_one = sums_copy(spot_x, first_half, got_x.at[first_half], beside)
    pass_z.wait()
    mate_d2.start()
    pass_x.wait()
    mate_d1.start()
    mate_z1.wait()
    mate_z2.wait()
    expert_step(spot_z)
    z_two = sums_copy(spot_z, second_half, got_z.at[second_half], above)
    mate_d1.wait()
    mate_d2.wait()
    expert_step(spot_d)
    d_one = sums_copy(spot_d, first_half, diag_x, beside)
    d_two = sums_copy(spot_d, second_half, diag_z, above)
    stores[1].start()
    stores[2].start()
    d_one.wait()
    sums_s[spot_z, :HALF] = (sums_s[spot_z, :HALF].astype(F32) + diag_x[...].astype(F32)).astype(
        BF
    )
    z_one = sums_copy(spot_z, first_half, got_z.at[first_half], above)
    d_two.wait()
    sums_s[spot_x, HALF:] = (sums_s[spot_x, HALF:].astype(F32) + diag_z[...].astype(F32)).astype(
        BF
    )
    x_two = sums_copy(spot_x, second_half, got_x.at[second_half], beside)
    for copy in (x_one, z_two, z_one, x_two):
        copy.wait()
    total = sums_s[spot].astype(F32) + got_x[...].astype(F32) + got_z[...].astype(F32)
    total = total.astype(BF)
    for side in range(2):
        slots = dot(choose[...], total[HALF * side : HALF * side + HALF], ((0,), (0,)))
        back_s[side] = slots.astype(BF).reshape(8, SLOT, 768)
    for_range(1, EXPERTS, lambda j: copy_r(next_group(j)).start())
    back_in[expert] = back_s[0, own_place]
    for_range(1, EXPERTS, lambda j: come_back(next_group(j)).wait_recv())
    for_range(1, EXPERTS, lambda j: copy_r(next_group(j)).wait_send())

    flat = rows_of(back_in)
    expert_y = dot(pick_row, flat)
    slot_grad = dot(pick_grad, flat)
    after = after_s[...]
    grad_gate = kept * jnp.sum(grad * expert_y, axis=-1, keepdims=True)
    grad_logits = ((grad_gate * gates) * (hot.astype(F32) - router_probs)).astype(BF)
    grad_normed = dot(grad_logits, router, ((1,), (1,))) + slot_grad
    scale = rms_scale(after)
    grad_after = grad + rms_back(grad_normed, after, scale, gain_two)
    grad_after_s[...] = grad_after
    grad_low[m] = grad_after.astype(BF)
    low_copies = gather_four(grad_low)
    low_copies[1].start()
    low_copies[0].start()
    result_s[...] = (after + (kept * gates) * expert_y).astype(BF)
    stores[0].start()
    grad_router = dot(grad_logits, normed_two_s[...], ((0,), (0,)))
    grad_gain_two = jnp.sum(grad_normed * after * scale, axis=0, keepdims=True)
    finish_four(low_copies)

    grad_proj = grad_low[...].reshape(512, 768)
    grad_mixed = dot(grad_proj, out_mine, ((1,), (1,))).astype(BF)
    grad_out = dot(mixed_s[...], grad_proj, ((0,), (0,)))
    grad_out_s[...] = grad_out.astype(BF).reshape(8, 24, 768)
    base_gs, base_gr = links.pair(8), links.pair(32)

    def copy_go(q):
        p = 8 * m + q
        return pltpu.make_async_remote_copy(
            src_ref=grad_out_s.at[q],
            dst_ref=grad_out_in.at[g],
            send_sem=send_sem.at[base_gs + q],
            recv_sem=recv_sem.at[base_gr + lax.rem(p - g + 32, 32)],
            device_id=coords(4 * p + m),
            device_id_type=MESH,
        )

    def away(q, fn):
        @pl.when(8 * m + q != g)
        def _():
            fn(q)

    for_range(0, 8, lambda q: away(q, lambda k: copy_go(k).start()))
    flip = ones_where(iota((256, 256), 0) + iota((256, 256), 1) == 255)
    pieces = [[[], [], []], [[], [], []]]
    sums = []
    for h in range(3):
        mirrored = jnp.zeros((256, 256), F32)
        for s in range(2):
            rows = slice(256 * s, 256 * s + 256)
            query = proj_s[rows, 64 * h : 64 * h + 64]
            key = proj_s[rows, 192 + 64 * h : 256 + 64 * h]
            value = proj_s[rows, 384 + 64 * h : 448 + 64 * h]
            grad_rows = grad_mixed[rows, 64 * h : 64 * h + 64]
            probs = probs_s[3 * s + h]
            grad_probs = dot(grad_rows, value, ((1,), (1,)))
            inner = jnp.sum(probs * grad_probs, axis=-1, keepdims=True)
            grad_scores = (probs * (grad_probs - inner)).astype(BF)
            mirrored = mirrored + dot(flip, grad_scores)
            pieces[s][0].append(dot(grad_scores, key).astype(BF))
            pieces[s][1].append(dot(grad_scores, query, ((0,), (0,))).astype(BF))
            pieces[s][2].append(dot(probs.astype(BF), grad_rows, ((0,), (0,))).astype(BF))
        line = jnp.concatenate([mirrored, jnp.zeros((256, 256), F32)], axis=1)
        line = pltpu.roll(line, 0, 1, stride=1, stride_axis=0)
        sums.append(jnp.sum(line, axis=0, keepdims=True))
    grad_heads = jnp.concatenate(
        [jnp.concatenate([p for part_of in s for p in part_of], axis=1) for s in pieces], axis=0
    )
    sums = jnp.concatenate(sums + [jnp.zeros((5, 512), F32)], axis=0)
    high = sums.astype(BF)
    rest = sums - high.astype(F32)
    middle = rest.astype(BF)
    low = (rest - middle.astype(F32)).astype(BF)
    grad_table = dot(
        jnp.concatenate([high.astype(F32), middle.astype(F32), low.astype(F32)], axis=0).astype(BF),
        in_bucket[...],
        ((1,), (1,)),
    )
    grad_table = (grad_table[16:24] + grad_table[8:16]) + grad_table[0:8]
    grad_table = jnp.sum(grad_table * head_row, axis=0, keepdims=True)
    lines = jnp.concatenate(
        [
            grad_router,
            jnp.zeros((1, 768), F32),
            grad_gain_two,
            grad_table,
            jnp.zeros((45, 768), F32),
        ],
        axis=0,
    )
    grad_qkv = dot(normed_s[...], grad_heads, ((0,), (0,)))
    grad_wide[...] = (
        jnp.concatenate([grad_qkv, lines.T], axis=1).reshape(32, 24, 640).astype(BF)
    )
    base_w = links.pair(32)

    def copy_w(j):
        p = lax.rem(g + j, 32)
        return links.copy(base_w + j, grad_wide.at[p], grad_wide_in.at[g], 4 * p + m)

    for_range(1, 32, lambda j: copy_w(j).start())
    grad_normed = dot(grad_heads, weights_s[:, :576], ((1,), (1,)))
    part[1] = grad_normed.astype(BF).reshape(4, 128, 768)
    copies = reduce_start(1)
    grad_wide_in[g] = grad_wide[g]
    reduce_pass(1, copies)
    values = x[...].astype(F32)
    grad_input_o[...] = (
        grad_after_s[...] + rms_back(reduce_end(1, copies), values, rms_scale(values), gain_one)
    ).astype(BF)
    for_range(0, 8, lambda q: away(q, lambda k: copy_go(k).wait_send()))

    @pl.when(plane == m)
    def _():
        grad_out_in[g] = grad_out_s[place]

        def take(j):
            sender = lax.rem(g - j + 32, 32)
            pltpu.make_async_remote_copy(
                src_ref=grad_out_s.at[0],
                dst_ref=grad_out_in.at[sender],
                send_sem=send_sem.at[base_gs],
                recv_sem=recv_sem.at[base_gr + j],
                device_id=coords(4 * sender + m),
                device_id_type=MESH,
            ).wait_recv()

        for_range(1, 32, take)
        lay_b[...] = jnp.sum(grad_out_in[...].astype(F32), axis=0)

    for_range(1, 32, lambda j: copy_w(j).wait())
    lay_a[...] = jnp.sum(grad_wide_in[...].astype(F32), axis=0)

    for store in stores:
        store.wait()

    for k in range(4):
        fin[k, 0:6, 0:640] = lay_a[6 * k : 6 * k + 6]
        fin[k, 0:6, 640:1408] = lay_b[6 * k : 6 * k + 6]
    base_f = links.pair(4)

    def copy_f(j):
        k = lax.rem(m + j, 4)
        return links.copy(base_f + j, fin.at[k], fin_in.at[m], quad + k)

    for j in range(1, 4):
        copy_f(j).start()
    fin_in[m] = fin[m]
    for j in range(1, 4):
        copy_f(j).wait()
    grad_qkv = jnp.concatenate(
        [fin_in[k, 0:6, 192 * i : 192 * i + 192] for i in range(3) for k in range(4)], axis=1
    )
    grad_qkv_o[...] = grad_qkv
    by_row = jnp.sum(grad_qkv * qkv[...].astype(F32), axis=1, keepdims=True)
    by_row = by_row / columns_of[0:6, 0:1]
    grad_out_o[...] = fin_in[plane, 0:6, 640:1408]
    total = jnp.sum(fin_in[:, 0:6, 512:640], axis=0)
    total = jnp.where(iota((6, 128), 1) == 80, by_row, total)
    grad_small_o[...] = jnp.concatenate([total, jnp.zeros((2, 128), F32)], axis=0)


def results_kernel(
    result,
    grad_input,
    grad_qkv,
    grad_out,
    grad_small,
    grad_in,
    grad_eout,
    result_o,
    grad_input_o,
    grad_qkv_o,
    grad_out_o,
    grad_router_o,
    gain_one_o,
    gain_two_o,
    bias_o,
    grad_in_o,
    grad_eout_o,
    sems,
):
    whole = [
        (grad_in, grad_in_o),
        (grad_eout, grad_eout_o),
        (result, result_o),
        (grad_input, grad_input_o),
        (grad_qkv, grad_qkv_o),
        (grad_out, grad_out_o),
    ]
    copies = [
        pltpu.make_async_copy(source, target, sems.at[i])
        for i, (source, target) in enumerate(whole)
    ]
    for copy in copies:
        copy.start()
    values = grad_small[...]
    grad_router_o[...] = values[0:6, 64:80]
    lines = jnp.concatenate([values, jnp.zeros((120, 128), F32)], axis=0).T
    gain_one_o[...] = lines[80:81, 0:6]
    gain_two_o[...] = lines[81:82, 0:6]
    bias_o[...] = lines[82:83, 0:3]
    for copy in copies:
        copy.wait()


def choose_matrix():
    choose = np.zeros((HALF, 8 * SLOT), np.float32)
    for kind in range(2):
        for source in range(8):
            for slot in range(CAP):
                choose[kind * 80 + source * CAP + slot, source * SLOT + kind * CAP + slot] = 1.0
    return choose


def shape(*dims, dtype=BF):
    return jax.ShapeDtypeStruct(dims, dtype)


SCRATCH = [
    ((128, 768), BF),
    ((1, 128), jnp.int32),
    ((1, 128), jnp.int32),
    ((1, 511), jnp.int32),
    ((6, 2304), BF),
    ((6, 768), BF),
    ((6, 16), BF),
    ((1, 6), BF),
    ((1, 6), BF),
    ((1, 3), BF),
    ((128, 768), BF),
    ((768, 384), BF),
    ((384, 768), BF),
    ((HALF, 8 * SLOT), BF),
    ((128, 768), BF),
    ((768, 384), F32),
    ((384, 768), F32),
    ((1, 512), jnp.int32),
    ((8, 128), F32),
    ((4, 16, 640), BF),
    ((4, 16, 640), BF),
    ((16, 768), BF),
    ((4, 16, 768), BF),
    ((24, 640), F32),
    ((24, 768), F32),
    ((24, 640), BF),
    ((24, 768), BF),
    ((32, 24, 640), BF),
    ((768, 640), BF),
    ((768, 512), BF),
    ((8, 24, 768), BF),
    ((4, 128, 768), BF),
    ((512, 768), BF),
    ((512, 576), BF),
    ((6, 256, 256), F32),
    ((512, 192), BF),
    ((2, 4, 128, 768), BF),
    ((2, 128, 768), BF),
    ((2, 128, 768), BF),
    ((2, 128, 768), BF),
    ((2, 128, 768), BF),
    ((128, 768), F32),
    ((128, 768), BF),
    ((EXPERTS, SLOT, 768), BF),
    ((2, 8, SLOT, 768), BF),
    ((4, 2, DEPTH, 768), BF),
    ((4, 2, DEPTH, 768), BF),
    ((4, DEPTH, 768), BF),
    ((4, DEPTH, 768), BF),
    ((DEPTH, 768), BF),
    ((DEPTH, 768), BF),
    ((HALF, 768), BF),
    ((HALF, 768), BF),
    ((2, 8, SLOT, 768), BF),
    ((EXPERTS, SLOT, 768), BF),
    ((128, 768), F32),
    ((4, 128, 768), BF),
    ((32, 24, 640), BF),
    ((32, 24, 640), BF),
    ((8, 24, 768), BF),
    ((32, 24, 768), BF),
    ((4, 8, 1408), F32),
    ((4, 8, 1408), F32),
]
TRANSFERS = 256


def body(
    inputs,
    cotangent,
    routes,
    drop_mask,
    buckets,
    qkv_weight,
    out_weight,
    router_weight,
    attn_gain,
    ffn_gain,
    bias_table,
    expert_in,
    expert_out,
):
    vmem = pl.BlockSpec(memory_space=pltpu.VMEM)
    anywhere = pl.BlockSpec(memory_space=pl.ANY)
    outputs = pl.pallas_call(
        layer_kernel,
        out_shape=[
            shape(128, 768),
            shape(6, 2304, dtype=F32),
            shape(6, 768, dtype=F32),
            shape(8, 128, dtype=F32),
            shape(128, 768),
            shape(768, 384, dtype=F32),
            shape(384, 768, dtype=F32),
        ],
        in_specs=[pl.BlockSpec(memory_space=pltpu.HBM)] * 14,
        out_specs=[vmem] * 4 + [anywhere] * 3,
        scratch_shapes=[pltpu.VMEM(dims, dtype) for dims, dtype in SCRATCH]
        + [
            pltpu.SemaphoreType.DMA((TRANSFERS,)),
            pltpu.SemaphoreType.DMA((TRANSFERS,)),
            pltpu.SemaphoreType.DMA((17,)),
        ],
        compiler_params=pltpu.CompilerParams(
            collective_id=0, has_side_effects=True, vmem_limit_bytes=60 * 1024 * 1024
        ),
    )(
        inputs,
        routes.reshape(1, 128),
        drop_mask.reshape(1, 128),
        buckets.reshape(1, 511),
        qkv_weight,
        out_weight,
        router_weight,
        attn_gain.reshape(1, 6),
        ffn_gain.reshape(1, 6),
        bias_table.reshape(1, 3),
        cotangent,
        expert_in,
        expert_out,
        jnp.asarray(choose_matrix(), BF),
    )
    grad_input, grad_qkv, grad_out, grad_small, result, grad_in, grad_eout = outputs
    final = pl.pallas_call(
        results_kernel,
        out_shape=[
            shape(128, 768),
            shape(128, 768),
            shape(6, 2304, dtype=F32),
            shape(6, 768, dtype=F32),
            shape(6, 16, dtype=F32),
            shape(1, 6, dtype=F32),
            shape(1, 6, dtype=F32),
            shape(1, 3, dtype=F32),
            shape(768, 384, dtype=F32),
            shape(384, 768, dtype=F32),
        ],
        in_specs=[vmem] * 7,
        out_specs=[anywhere] * 4 + [vmem] * 4 + [anywhere] * 2,
        scratch_shapes=[pltpu.SemaphoreType.DMA((6,))],
        compiler_params=pltpu.CompilerParams(vmem_limit_bytes=60 * 1024 * 1024),
    )(result, grad_input, grad_qkv, grad_out, grad_small, grad_in, grad_eout)
    return (
        *final[:5],
        final[5].reshape(6),
        final[6].reshape(6),
        final[7].reshape(3),
        *final[8:],
    )


def solution(mesh):
    placed = (
        P(("fsdp", "sp"), None),
        P(("fsdp", "sp"), None),
        P(("fsdp", "sp"), None),
        P(("fsdp", "sp")),
        P(),
        P(("fsdp", "sp"), None),
        P(("fsdp", "sp"), None),
        P(("fsdp", "sp"), None),
        P(("fsdp", "sp")),
        P(("fsdp", "sp")),
        P(("fsdp", "sp")),
        P(None, ("fsdp", "sp")),
        P(("fsdp", "sp"), None),
    )
    return jax.shard_map(
        body,
        mesh=mesh,
        in_specs=placed,
        out_specs=(
            P(("fsdp", "sp"), None),
            P(("fsdp", "sp"), None),
            P(("fsdp", "sp"), None),
            P(("fsdp", "sp"), None),
            P(("fsdp", "sp"), None),
            P(("fsdp", "sp")),
            P(("fsdp", "sp")),
            P(("fsdp", "sp")),
            P(None, ("fsdp", "sp")),
            P(("fsdp", "sp"), None),
        ),
        check_vma=False,
    )
```

```python
import functools

import jax
import jax.numpy as jnp
import numpy as np
from jax import lax
from jax.experimental import pallas as pl
from jax.experimental.pallas import tpu as pltpu
from jax.sharding import PartitionSpec as P

HEADS = 12
HEAD_DIM = 64
EXPERTS = 16
BUCKETS = 32
CAP = 10
EPSILON = 1e-06
MESH = pl.DeviceIdType.MESH
BF = jnp.bfloat16
F32 = jnp.float32
SLOT = 24
GELU_C = 0.7978845608028654
GELU_A = 0.044715
DEPTH = 2 * EXPERTS * CAP
HALF = EXPERTS * CAP


def coords(flat):
    return (lax.div(flat, 2), lax.rem(flat, 2))


def for_range(low, high, fn):
    def step(j, carry):
        fn(j)
        return carry

    lax.fori_loop(low, high, step, 0)


def dot(a, b, dims=((1,), (0,)), precision=None):
    return lax.dot_general(
        a, b, (dims, ((), ())), precision=precision, preferred_element_type=F32
    )


def rms_scale(values):
    return lax.rsqrt(jnp.mean(values * values, axis=-1, keepdims=True) + EPSILON)


def rms_back(grad, values, scale, gain):
    weighted = grad * gain
    inner = jnp.mean(weighted * values, axis=-1, keepdims=True)
    return scale * weighted - values * (scale * scale * scale * inner)


def iota(shape, dim):
    return lax.broadcasted_iota(jnp.int32, shape, dim)


def ones_where(mask):
    return mask.astype(F32).astype(BF)


class Links:
    def __init__(self, send, recv):
        self.send, self.recv, self.used = send, recv, 0

    def pair(self, count=1):
        first = self.used
        self.used += count
        return first

    def copy(self, index, source, target, device):
        return pltpu.make_async_remote_copy(
            src_ref=source,
            dst_ref=target,
            send_sem=self.send.at[index],
            recv_sem=self.recv.at[index],
            device_id=coords(device),
            device_id_type=MESH,
        )


def rows_of(ref):
    blocks, rows, width = ref.shape
    return ref[...].astype(F32).reshape(blocks * rows, width).astype(BF)


def layer_kernel(
    x_any,
    routes_any,
    drop_any,
    buckets_any,
    qkv_any,
    out_w_any,
    router_w_any,
    gain_attn_any,
    gain_ffn_any,
    bias_w_any,
    cot_any,
    expert_in_any,
    expert_out_any,
    choose_any,
    grad_input_any,
    grad_qkv_o,
    grad_out_o,
    grad_small_o,
    result_any,
    grad_in_any,
    grad_eout_any,
    x,
    routes,
    drop,
    buckets,
    qkv,
    out_w,
    router_w,
    gain_attn,
    gain_ffn,
    bias_w,
    cot,
    expert_in,
    expert_out,
    choose,
    result_s,
    grad_input_s,
    grad_in_o,
    grad_eout_o,
    offsets,
    lines_s,
    packs,
    packs_in,
    rawb,
    rawb_in,
    lay_a,
    lay_b,
    chunk_a,
    chunk_b,
    wide,
    weights_s,
    in_bucket,
    outs,
    tokens,
    normed_s,
    proj_s,
    probs_s,
    mixed_s,
    part,
    from_mate,
    merge,
    to_x,
    from_x,
    after_s,
    normed_two_s,
    send_s,
    arrived,
    rows_s,
    parts_s,
    mate_parts,
    sums_s,
    got_x,
    got_z,
    diag_x,
    diag_z,
    back_s,
    back_in,
    grad_after_s,
    grad_low,
    grad_wide,
    grad_wide_in,
    grad_out_s,
    grad_out_in,
    fin,
    fin_in,
    send_sem,
    recv_sem,
    local_sem,
):
    loads = [
        pltpu.make_async_copy(source, target, local_sem.at[i])
        for i, (source, target) in enumerate(
            [
                (cot_any, cot),
                (expert_in_any, expert_in),
                (expert_out_any, expert_out),
                (choose_any, choose),
            ]
        )
    ]
    early = [
        pltpu.make_async_copy(source, target, local_sem.at[7 + i])
        for i, (source, target) in enumerate(
            [
                (x_any, x),
                (routes_any, routes),
                (drop_any, drop),
                (buckets_any, buckets),
                (qkv_any, qkv),
                (out_w_any, out_w),
                (router_w_any, router_w),
                (gain_attn_any, gain_attn),
                (gain_ffn_any, gain_ffn),
                (bias_w_any, bias_w),
            ]
        )
    ]
    stores = [
        pltpu.make_async_copy(source, target, local_sem.at[4 + i])
        for i, (source, target) in enumerate(
            [(result_s, result_any), (grad_in_o, grad_in_any), (grad_eout_o, grad_eout_any)]
        )
    ]
    last_store = pltpu.make_async_copy(grad_input_s, grad_input_any, local_sem.at[17])
    links = Links(send_sem, recv_sem)
    fs, sp = lax.axis_index("fsdp"), lax.axis_index("sp")
    f = fs * 2 + sp
    m, g = lax.rem(f, 4), lax.div(f, 4)
    plane, place = lax.div(g, 8), lax.rem(g, 8)
    core, x_lo = lax.div(m, 2), lax.rem(m, 2)
    expert, member = lax.div(f, 8), lax.rem(f, 8)
    z_lo = lax.div(member, 4)
    x_hi, own_place = lax.rem(lax.div(expert, 2), 2), lax.div(expert, 4) * 2 + lax.rem(expert, 2)

    def side_of(k):
        return lax.rem(lax.rem(lax.div(k, 2), 2) + x_hi, 2)

    def place_in(k):
        return lax.div(k, 4) * 2 + lax.rem(k, 2)

    quad = f - m
    mate_m = (1 - core) * 2 + x_lo
    beside_m = core * 2 + (1 - x_lo)
    cross_m = (1 - core) * 2 + (1 - x_lo)
    mate, beside = quad + mate_m, quad + beside_m
    above = f - z_lo * 4 + (1 - z_lo) * 4
    spot = z_lo * 2 + x_lo
    spot_x = z_lo * 2 + (1 - x_lo)
    spot_z = (1 - z_lo) * 2 + x_lo
    spot_d = (1 - z_lo) * 2 + (1 - x_lo)

    barrier = pltpu.get_barrier_semaphore()

    def hello(device):
        pl.semaphore_signal(barrier, inc=1, device_id=coords(device), device_id_type=MESH)

    for j in range(1, 4):
        hello(quad + lax.rem(m + j, 4))
    for_range(1, 32, lambda j: hello(4 * lax.rem(g + j, 32) + m))

    for load in early:
        load.start()
    for load in loads:
        load.start()
    for load in early:
        load.wait()
    tokens[m] = x[...]
    offsets[...] = jnp.full((1, 512), -1, jnp.int32)
    offsets[:, :511] = buckets[...]
    lines_s[...] = jnp.zeros((8, 128), F32)
    lines_s[0:1, 0:6] = gain_attn[...].astype(F32)
    lines_s[1:2, 0:6] = gain_ffn[...].astype(F32)
    lines_s[2:3, 0:3] = bias_w[...].astype(F32)
    lines_s[3:4] = routes[...].astype(F32)
    lines_s[4:5] = drop[...].astype(F32)
    columns_of = lines_s[...].T
    chosen = columns_of[:, 3:4].astype(jnp.int32)
    kept = columns_of[:, 4:5]
    weight = qkv[...].astype(F32)
    extra = jnp.concatenate(
        [router_w[...].astype(F32), columns_of[:6], jnp.zeros((6, 40), F32)], axis=1
    )
    for k in range(4):
        columns = [weight[:, 768 * i + 192 * k : 768 * i + 192 * k + 192] for i in range(3)]
        packs[k, 0:6] = jnp.concatenate(columns + [extra], axis=1).astype(BF)
    rawb[0:6] = out_w[...]
    pl.semaphore_wait(barrier, 34)

    base_p, base_b = links.pair(4), links.pair(4)

    def copy_pack(j):
        k = lax.rem(m + j, 4)
        return links.copy(base_p + j, packs.at[k], packs_in.at[m], quad + k)

    def copy_raw(j):
        return links.copy(base_b + j, rawb, rawb_in.at[m], quad + lax.rem(m + j, 4))

    for j in range(1, 4):
        copy_pack(j).start()
        copy_raw(j).start()
    packs_in[m] = packs[m]
    rawb_in[m] = rawb[...]

    def gather_four(buffer):
        first = links.pair(3)
        to_mate = links.copy(first, buffer.at[m], buffer.at[m], mate)
        to_beside = links.copy(first + 1, buffer.at[m], buffer.at[m], beside)
        passed = links.copy(first + 2, buffer.at[beside_m], buffer.at[beside_m], mate)
        return to_mate, to_beside, passed

    def finish_four(copies):
        to_mate, to_beside, passed = copies
        to_beside.wait_recv()
        passed.start()
        to_mate.wait()
        to_beside.wait_send()
        passed.wait()

    token_copies = gather_four(tokens)
    token_copies[1].start()
    token_copies[0].start()
    for j in range(1, 4):
        copy_pack(j).wait()
        copy_raw(j).wait()
    for k in range(4):
        lay_a[6 * k : 6 * k + 6] = packs_in[k].astype(F32)[0:6]
        lay_b[6 * k : 6 * k + 6] = rawb_in[k].astype(F32)[0:6]
    chunk_a[...] = lay_a[...].astype(BF)
    chunk_b[...] = lay_b[...].astype(BF)

    base_a = links.pair(32)
    base_o, base_r = links.pair(32), links.pair(8)

    def copy_a(j):
        return links.copy(base_a + j, chunk_a, wide.at[g], 4 * lax.rem(g + j, 32) + m)

    def copy_b(j, q):
        return pltpu.make_async_remote_copy(
            src_ref=chunk_b,
            dst_ref=outs.at[q],
            send_sem=send_sem.at[base_o + j],
            recv_sem=recv_sem.at[base_r + q],
            device_id=coords(4 * lax.rem(g + j, 32) + m),
            device_id_type=MESH,
        )

    for_range(1, 32, lambda j: copy_a(j).start())

    @pl.when(plane == m)
    def _():
        for_range(1, 32, lambda j: copy_b(j, place).start())
        outs[place] = chunk_b[...]

    wide[g] = chunk_a[...]
    finish_four(token_copies)
    values = tokens[...].astype(F32).reshape(512, 768)
    scaled = values * rms_scale(values)
    head_row = (iota((32, 24, 128), 1).reshape(768, 128) == 6 * m + iota((768, 128), 1)).astype(F32)
    head_row = jnp.where(iota((8, 768), 0) < 3, head_row.T[:8], 0.0)
    in_bucket[...] = ones_where(iota((32, 24, 512), 0).reshape(768, 512) == offsets[...])
    for_range(1, 32, lambda j: copy_a(j).wait())

    weights_s[...] = rows_of(wide)
    weights = weights_s[...]
    turned = weights[:, 512:640].astype(F32).T
    gain_one, gain_two, table = turned[80:81], turned[81:82], turned[82:83]
    router = weights[:, 576:592]
    by_offset = dot((head_row * table).astype(BF), in_bucket[...])
    normed = (scaled * gain_one).astype(BF)
    normed_s[...] = normed
    proj = dot(normed, weights[:, :576]).astype(BF)
    proj_s[...] = proj
    seqs = [[], []]
    for h in range(3):
        line = jnp.broadcast_to(by_offset[h : h + 1], (256, 512))
        bias = pltpu.roll(line, 257, 1, stride=1, stride_axis=0)[:, :256]
        for s in range(2):
            rows = slice(256 * s, 256 * s + 256)
            query = proj[rows, 64 * h : 64 * h + 64]
            key = proj[rows, 192 + 64 * h : 256 + 64 * h]
            value = proj[rows, 384 + 64 * h : 448 + 64 * h]
            scores = dot(query, key, ((1,), (1,))) + bias
            exponent = jnp.exp(scores - jnp.max(scores, axis=-1, keepdims=True))
            probs = exponent * (1.0 / jnp.sum(exponent, axis=-1, keepdims=True))
            probs_s[3 * s + h] = probs
            seqs[s].append(dot(probs.astype(BF), value).astype(BF))
    mixed = jnp.concatenate([jnp.concatenate(s, axis=1) for s in seqs], axis=0)
    mixed_s[...] = mixed

    def take_b(q):
        @pl.when(8 * m + q != g)
        def _():
            copy_b(1, q).wait_recv()

    for_range(0, 8, take_b)

    @pl.when(plane == m)
    def _():
        for_range(1, 32, lambda j: copy_b(j, place).wait_send())

    out_mine = rows_of(outs)
    part[0] = dot(mixed, out_mine).astype(BF).reshape(4, 128, 768)

    def reduce_start(n):
        first = links.pair(3)
        cross = links.copy(first, part.at[n, cross_m], merge.at[n], mate)
        straight = links.copy(first + 1, part.at[n, mate_m], from_mate.at[n], mate)
        over = links.copy(first + 2, to_x.at[n], from_x.at[n], beside)
        cross.start()
        straight.start()
        return cross, straight, over

    def reduce_pass(n, copies):
        cross, straight, over = copies
        cross.wait()
        to_x[n] = (part[n, beside_m].astype(F32) + merge[n].astype(F32)).astype(BF)
        over.start()

    def reduce_end(n, copies):
        cross, straight, over = copies
        straight.wait()
        over.wait()
        return part[n, m].astype(F32) + from_mate[n].astype(F32) + from_x[n].astype(F32)

    copies = reduce_start(0)
    reduce_pass(0, copies)
    hot = chosen == iota((128, EXPERTS), 1)
    earlier = iota((128, 128), 1) < iota((128, 128), 0)
    counts = dot(ones_where(earlier), ones_where(hot))
    slot = jnp.sum(jnp.where(hot, counts, 0.0), axis=-1, keepdims=True).astype(jnp.int32)
    target = jnp.where(kept > 0, chosen * SLOT + slot, -SLOT)
    lanes = iota((128, EXPERTS * SLOT), 1)
    pick_row, pick_grad = ones_where(lanes == target), ones_where(lanes == target + CAP)
    loads[0].wait()
    grad = cot[...].astype(F32)
    after = x[...].astype(F32) + reduce_end(0, copies)
    after_s[...] = after
    normed_two = (after * rms_scale(after) * gain_two).astype(BF)
    normed_two_s[...] = normed_two
    logits = dot(normed_two, router)
    exponent = jnp.exp(logits - jnp.max(logits, axis=-1, keepdims=True))
    router_probs = exponent / jnp.sum(exponent, axis=-1, keepdims=True)
    gates = jnp.sum(jnp.where(hot, router_probs, 0.0), axis=-1, keepdims=True)
    grad_y = (grad * (kept * gates)).astype(BF)
    slots = dot(
        jnp.concatenate([pick_row, pick_grad], axis=0),
        jnp.concatenate([normed_two, grad_y], axis=0),
        ((0,), (0,)),
    )
    send_s[...] = slots.astype(BF).reshape(EXPERTS, SLOT, 768)

    base_d, base_r = links.pair(EXPERTS), links.pair(EXPERTS)

    def group_at(side, i):
        return (lax.div(i, 2) * 2 + lax.rem(side + x_hi, 2)) * 2 + lax.rem(i, 2)

    def pair_copy(base, k, source, target):
        return pltpu.make_async_remote_copy(
            src_ref=source,
            dst_ref=target,
            send_sem=send_sem.at[base + k],
            recv_sem=recv_sem.at[base + expert],
            device_id=coords(8 * k + member),
            device_id_type=MESH,
        )

    def copy_d(k):
        return pair_copy(base_d, k, send_s.at[k], arrived.at[side_of(k), own_place])

    def arrival(side, i):
        k = group_at(side, i)
        return links.copy(base_d + k, send_s.at[k], arrived.at[side, i], 8 * k + member)

    def copy_r(k):
        return pair_copy(base_r, k, back_s.at[side_of(k), place_in(k)], back_in.at[expert])

    def come_back(k):
        return links.copy(base_r + k, back_s.at[0, 0], back_in.at[k], 8 * k + member)

    def next_group(j):
        return lax.rem(expert + j, EXPERTS)

    for_range(1, EXPERTS, lambda j: copy_d(next_group(j)).start())
    arrived[0, own_place] = send_s[expert]
    grad_in_o[...] = jnp.zeros_like(grad_in_o)
    grad_eout_o[...] = jnp.zeros_like(grad_eout_o)
    loads[3].wait()

    def take_rows(side):
        def take(i):
            if side == 0:
                pl.when(i != own_place)(lambda: arrival(side, i).wait_recv())
            else:
                arrival(side, i).wait_recv()

        for_range(0, 8, take)
        rows_s[spot, core, HALF * side : HALF * side + HALF] = dot(
            choose[...], rows_of(arrived.at[side])
        ).astype(BF)

    first_half, second_half = pl.ds(0, HALF), pl.ds(HALF, HALF)

    def rows_copy(place_of, half, device):
        ref = rows_s.at[place_of, core, half]
        return links.copy(links.pair(), ref, ref, device)

    out_x2 = rows_copy(spot, second_half, beside)
    out_z1 = rows_copy(spot, first_half, above)
    out_x1 = rows_copy(spot, first_half, beside)
    out_z2 = rows_copy(spot, second_half, above)
    out_m1 = rows_copy(spot, first_half, mate)
    out_m2 = rows_copy(spot, second_half, mate)
    pass_x = rows_copy(spot_z, first_half, beside)
    pass_z = rows_copy(spot_x, second_half, above)
    mate_x1, mate_x2 = (rows_copy(spot_x, h, mate) for h in (first_half, second_half))
    mate_z1, mate_z2 = (rows_copy(spot_z, h, mate) for h in (first_half, second_half))
    mate_d1, mate_d2 = (rows_copy(spot_d, h, mate) for h in (first_half, second_half))
    take_rows(0)
    for copy in (out_z1, out_x1, out_m1):
        copy.start()
    take_rows(1)
    for copy in (out_x2, out_z2, out_m2):
        copy.start()
    for_range(1, EXPERTS, lambda j: copy_d(next_group(j)).wait_send())

    def expert_step(place_of):
        both = rows_s[place_of]
        row = jnp.concatenate([both[:, :80], both[:, 160:240]], axis=1).reshape(DEPTH, 768)
        grad_row = jnp.concatenate([both[:, 80:160], both[:, 240:]], axis=1).reshape(DEPTH, 768)
        pre = dot(row, expert_in[...])
        square = pre * pre
        tanh = jnp.tanh(GELU_C * (pre + GELU_A * (pre * square)))
        half = 0.5 * (1.0 + tanh)
        act = (pre * half).astype(BF)
        slope = half + (0.5 * GELU_C) * pre * (1.0 - tanh * tanh) * (1.0 + 3.0 * GELU_A * square)
        out = dot(act, expert_out[...]).astype(BF).reshape(2, HALF, 768)
        parts_s[place_of, :, :80] = out[:, :80]
        parts_s[place_of, :, 160:240] = out[:, 80:]
        grad_act = dot(grad_row, expert_out[...], ((1,), (1,)))
        grad_pre = (grad_act * slope).astype(BF)
        out = dot(grad_pre, expert_in[...], ((1,), (1,))).astype(BF).reshape(2, HALF, 768)
        parts_s[place_of, :, 80:160] = out[:, :80]
        parts_s[place_of, :, 240:] = out[:, 80:]
        swap = links.copy(
            links.pair(), parts_s.at[place_of, 1 - core], mate_parts.at[place_of], mate
        )
        swap.start()
        grad_in_o[...] += dot(row, grad_pre, ((0,), (0,)))
        grad_eout_o[...] += dot(act, grad_row, ((0,), (0,)))
        swap.wait()
        sums_s[place_of] = (
            parts_s[place_of, core].astype(F32) + mate_parts[place_of].astype(F32)
        ).astype(BF)

    def sums_copy(place_of, half, target, device):
        copy = links.copy(links.pair(), sums_s.at[place_of, half], target, device)
        copy.start()
        return copy

    loads[1].wait()
    loads[2].wait()
    out_m1.wait()
    out_m2.wait()
    expert_step(spot)
    out_z1.wait()
    pass_x.start()
    mate_z1.start()
    out_x1.wait()
    mate_x1.start()
    out_x2.wait()
    pass_z.start()
    mate_x2.start()
    out_z2.wait()
    mate_z2.start()
    mate_x2.wait()
    mate_x1.wait()
    expert_step(spot_x)
    x_one = sums_copy(spot_x, first_half, got_x.at[first_half], beside)
    pass_z.wait()
    mate_d2.start()
    pass_x.wait()
    mate_d1.start()
    mate_z1.wait()
    mate_z2.wait()
    expert_step(spot_z)
    z_two = sums_copy(spot_z, second_half, got_z.at[second_half], above)
    mate_d1.wait()
    mate_d2.wait()
    expert_step(spot_d)
    d_one = sums_copy(spot_d, first_half, diag_x, beside)
    d_two = sums_copy(spot_d, second_half, diag_z, above)
    stores[1].start()
    stores[2].start()
    d_one.wait()
    sums_s[spot_z, :HALF] = (sums_s[spot_z, :HALF].astype(F32) + diag_x[...].astype(F32)).astype(
        BF
    )
    z_one = sums_copy(spot_z, first_half, got_z.at[first_half], above)
    d_two.wait()
    sums_s[spot_x, HALF:] = (sums_s[spot_x, HALF:].astype(F32) + diag_z[...].astype(F32)).astype(
        BF
    )
    x_two = sums_copy(spot_x, second_half, got_x.at[second_half], beside)
    for copy in (x_one, z_two, z_one, x_two):
        copy.wait()
    total = sums_s[spot].astype(F32) + got_x[...].astype(F32) + got_z[...].astype(F32)
    total = total.astype(BF)
    for side in range(2):
        slots = dot(choose[...], total[HALF * side : HALF * side + HALF], ((0,), (0,)))
        back_s[side] = slots.astype(BF).reshape(8, SLOT, 768)
    for_range(1, EXPERTS, lambda j: copy_r(next_group(j)).start())
    back_in[expert] = back_s[0, own_place]
    for_range(1, EXPERTS, lambda j: come_back(next_group(j)).wait_recv())
    for_range(1, EXPERTS, lambda j: copy_r(next_group(j)).wait_send())

    flat = rows_of(back_in)
    expert_y = dot(pick_row, flat)
    slot_grad = dot(pick_grad, flat)
    after = after_s[...]
    grad_gate = kept * jnp.sum(grad * expert_y, axis=-1, keepdims=True)
    grad_logits = ((grad_gate * gates) * (hot.astype(F32) - router_probs)).astype(BF)
    grad_normed = dot(grad_logits, router, ((1,), (1,))) + slot_grad
    scale = rms_scale(after)
    grad_after = grad + rms_back(grad_normed, after, scale, gain_two)
    grad_after_s[...] = grad_after
    grad_low[m] = grad_after.astype(BF)
    low_copies = gather_four(grad_low)
    low_copies[1].start()
    low_copies[0].start()
    result_s[...] = (after + (kept * gates) * expert_y).astype(BF)
    stores[0].start()
    grad_router = dot(grad_logits, normed_two_s[...], ((0,), (0,)))
    grad_gain_two = jnp.sum(grad_normed * after * scale, axis=0, keepdims=True)
    finish_four(low_copies)

    grad_proj = grad_low[...].reshape(512, 768)
    grad_mixed = dot(grad_proj, out_mine, ((1,), (1,))).astype(BF)
    grad_out = dot(mixed_s[...], grad_proj, ((0,), (0,)))
    grad_out_s[...] = grad_out.astype(BF).reshape(8, 24, 768)
    base_gs, base_gr = links.pair(8), links.pair(32)

    def copy_go(q):
        p = 8 * m + q
        return pltpu.make_async_remote_copy(
            src_ref=grad_out_s.at[q],
            dst_ref=grad_out_in.at[g],
            send_sem=send_sem.at[base_gs + q],
            recv_sem=recv_sem.at[base_gr + lax.rem(p - g + 32, 32)],
            device_id=coords(4 * p + m),
            device_id_type=MESH,
        )

    def away(q, fn):
        @pl.when(8 * m + q != g)
        def _():
            fn(q)

    for_range(0, 8, lambda q: away(q, lambda k: copy_go(k).start()))
    flip = ones_where(iota((256, 256), 0) + iota((256, 256), 1) == 255)
    pieces = [[[], [], []], [[], [], []]]
    sums = []
    for h in range(3):
        mirrored = jnp.zeros((256, 256), F32)
        for s in range(2):
            rows = slice(256 * s, 256 * s + 256)
            query = proj_s[rows, 64 * h : 64 * h + 64]
            key = proj_s[rows, 192 + 64 * h : 256 + 64 * h]
            value = proj_s[rows, 384 + 64 * h : 448 + 64 * h]
            grad_rows = grad_mixed[rows, 64 * h : 64 * h + 64]
            probs = probs_s[3 * s + h]
            grad_probs = dot(grad_rows, value, ((1,), (1,)))
            inner = jnp.sum(probs * grad_probs, axis=-1, keepdims=True)
            grad_scores = (probs * (grad_probs - inner)).astype(BF)
            mirrored = mirrored + dot(flip, grad_scores)
            pieces[s][0].append(dot(grad_scores, key).astype(BF))
            pieces[s][1].append(dot(grad_scores, query, ((0,), (0,))).astype(BF))
            pieces[s][2].append(dot(probs.astype(BF), grad_rows, ((0,), (0,))).astype(BF))
        line = jnp.concatenate([mirrored, jnp.zeros((256, 256), F32)], axis=1)
        line = pltpu.roll(line, 0, 1, stride=1, stride_axis=0)
        sums.append(jnp.sum(line, axis=0, keepdims=True))
    grad_heads = jnp.concatenate(
        [jnp.concatenate([p for part_of in s for p in part_of], axis=1) for s in pieces], axis=0
    )
    sums = jnp.concatenate(sums + [jnp.zeros((5, 512), F32)], axis=0)
    high = sums.astype(BF)
    rest = sums - high.astype(F32)
    middle = rest.astype(BF)
    low = (rest - middle.astype(F32)).astype(BF)
    grad_table = dot(
        jnp.concatenate([high.astype(F32), middle.astype(F32), low.astype(F32)], axis=0).astype(BF),
        in_bucket[...],
        ((1,), (1,)),
    )
    grad_table = (grad_table[16:24] + grad_table[8:16]) + grad_table[0:8]
    grad_table = jnp.sum(grad_table * head_row, axis=0, keepdims=True)
    lines = jnp.concatenate(
        [
            grad_router,
            jnp.zeros((1, 768), F32),
            grad_gain_two,
            grad_table,
            jnp.zeros((45, 768), F32),
        ],
        axis=0,
    )
    grad_qkv = dot(normed_s[...], grad_heads, ((0,), (0,)))
    grad_wide[...] = (
        jnp.concatenate([grad_qkv, lines.T], axis=1).reshape(32, 24, 640).astype(BF)
    )
    base_w = links.pair(32)

    def copy_w(j):
        p = lax.rem(g + j, 32)
        return links.copy(base_w + j, grad_wide.at[p], grad_wide_in.at[g], 4 * p + m)

    for_range(1, 32, lambda j: copy_w(j).start())
    grad_normed = dot(grad_heads, weights_s[:, :576], ((1,), (1,)))
    part[1] = grad_normed.astype(BF).reshape(4, 128, 768)
    copies = reduce_start(1)
    grad_wide_in[g] = grad_wide[g]
    reduce_pass(1, copies)
    values = x[...].astype(F32)
    grad_input_s[...] = (
        grad_after_s[...] + rms_back(reduce_end(1, copies), values, rms_scale(values), gain_one)
    ).astype(BF)
    last_store.start()
    for_range(0, 8, lambda q: away(q, lambda k: copy_go(k).wait_send()))

    @pl.when(plane == m)
    def _():
        grad_out_in[g] = grad_out_s[place]

        def take(j):
            sender = lax.rem(g - j + 32, 32)
            pltpu.make_async_remote_copy(
                src_ref=grad_out_s.at[0],
                dst_ref=grad_out_in.at[sender],
                send_sem=send_sem.at[base_gs],
                recv_sem=recv_sem.at[base_gr + j],
                device_id=coords(4 * sender + m),
                device_id_type=MESH,
            ).wait_recv()

        for_range(1, 32, take)
        lay_b[...] = jnp.sum(grad_out_in[...].astype(F32), axis=0)

    for_range(1, 32, lambda j: copy_w(j).wait())
    lay_a[...] = jnp.sum(grad_wide_in[...].astype(F32), axis=0)

    for store in stores + [last_store]:
        store.wait()

    for k in range(4):
        fin[k, 0:6, 0:640] = lay_a[6 * k : 6 * k + 6]
        fin[k, 0:6, 640:1408] = lay_b[6 * k : 6 * k + 6]
    base_f = links.pair(4)

    def copy_f(j):
        k = lax.rem(m + j, 4)
        return links.copy(base_f + j, fin.at[k], fin_in.at[m], quad + k)

    for j in range(1, 4):
        copy_f(j).start()
    fin_in[m] = fin[m]
    for j in range(1, 4):
        copy_f(j).wait()
    grad_qkv = jnp.concatenate(
        [fin_in[k, 0:6, 192 * i : 192 * i + 192] for i in range(3) for k in range(4)], axis=1
    )
    grad_qkv_o[...] = grad_qkv
    by_row = jnp.sum(grad_qkv * qkv[...].astype(F32), axis=1, keepdims=True)
    by_row = by_row / columns_of[0:6, 0:1]
    grad_out_o[...] = fin_in[plane, 0:6, 640:1408]
    total = jnp.sum(fin_in[:, 0:6, 512:640], axis=0)
    total = jnp.where(iota((6, 128), 1) == 80, by_row, total)
    grad_small_o[...] = jnp.concatenate([total, jnp.zeros((2, 128), F32)], axis=0)


def results_kernel(
    result,
    grad_input,
    grad_qkv,
    grad_out,
    grad_small,
    grad_in,
    grad_eout,
    result_o,
    grad_input_o,
    grad_qkv_o,
    grad_out_o,
    grad_router_o,
    gain_one_o,
    gain_two_o,
    bias_o,
    grad_in_o,
    grad_eout_o,
    sems,
):
    whole = [
        (grad_in, grad_in_o),
        (grad_eout, grad_eout_o),
        (result, result_o),
        (grad_input, grad_input_o),
        (grad_qkv, grad_qkv_o),
        (grad_out, grad_out_o),
    ]
    copies = [
        pltpu.make_async_copy(source, target, sems.at[i])
        for i, (source, target) in enumerate(whole)
    ]
    for copy in copies:
        copy.start()
    values = grad_small[...]
    grad_router_o[...] = values[0:6, 64:80]
    lines = jnp.concatenate([values, jnp.zeros((120, 128), F32)], axis=0).T
    gain_one_o[...] = lines[80:81, 0:6]
    gain_two_o[...] = lines[81:82, 0:6]
    bias_o[...] = lines[82:83, 0:3]
    for copy in copies:
        copy.wait()


def choose_matrix():
    choose = np.zeros((HALF, 8 * SLOT), np.float32)
    for kind in range(2):
        for source in range(8):
            for slot in range(CAP):
                choose[kind * 80 + source * CAP + slot, source * SLOT + kind * CAP + slot] = 1.0
    return choose


def shape(*dims, dtype=BF):
    return jax.ShapeDtypeStruct(dims, dtype)


SCRATCH = [
    ((128, 768), BF),
    ((1, 128), jnp.int32),
    ((1, 128), jnp.int32),
    ((1, 511), jnp.int32),
    ((6, 2304), BF),
    ((6, 768), BF),
    ((6, 16), BF),
    ((1, 6), BF),
    ((1, 6), BF),
    ((1, 3), BF),
    ((128, 768), BF),
    ((768, 384), BF),
    ((384, 768), BF),
    ((HALF, 8 * SLOT), BF),
    ((128, 768), BF),
    ((128, 768), BF),
    ((768, 384), F32),
    ((384, 768), F32),
    ((1, 512), jnp.int32),
    ((8, 128), F32),
    ((4, 16, 640), BF),
    ((4, 16, 640), BF),
    ((16, 768), BF),
    ((4, 16, 768), BF),
    ((24, 640), F32),
    ((24, 768), F32),
    ((24, 640), BF),
    ((24, 768), BF),
    ((32, 24, 640), BF),
    ((768, 640), BF),
    ((768, 512), BF),
    ((8, 24, 768), BF),
    ((4, 128, 768), BF),
    ((512, 768), BF),
    ((512, 576), BF),
    ((6, 256, 256), F32),
    ((512, 192), BF),
    ((2, 4, 128, 768), BF),
    ((2, 128, 768), BF),
    ((2, 128, 768), BF),
    ((2, 128, 768), BF),
    ((2, 128, 768), BF),
    ((128, 768), F32),
    ((128, 768), BF),
    ((EXPERTS, SLOT, 768), BF),
    ((2, 8, SLOT, 768), BF),
    ((4, 2, DEPTH, 768), BF),
    ((4, 2, DEPTH, 768), BF),
    ((4, DEPTH, 768), BF),
    ((4, DEPTH, 768), BF),
    ((DEPTH, 768), BF),
    ((DEPTH, 768), BF),
    ((HALF, 768), BF),
    ((HALF, 768), BF),
    ((2, 8, SLOT, 768), BF),
    ((EXPERTS, SLOT, 768), BF),
    ((128, 768), F32),
    ((4, 128, 768), BF),
    ((32, 24, 640), BF),
    ((32, 24, 640), BF),
    ((8, 24, 768), BF),
    ((32, 24, 768), BF),
    ((4, 8, 1408), F32),
    ((4, 8, 1408), F32),
]
TRANSFERS = 256


def body(
    inputs,
    cotangent,
    routes,
    drop_mask,
    buckets,
    qkv_weight,
    out_weight,
    router_weight,
    attn_gain,
    ffn_gain,
    bias_table,
    expert_in,
    expert_out,
):
    vmem = pl.BlockSpec(memory_space=pltpu.VMEM)
    anywhere = pl.BlockSpec(memory_space=pl.ANY)
    outputs = pl.pallas_call(
        layer_kernel,
        out_shape=[
            shape(128, 768),
            shape(6, 2304, dtype=F32),
            shape(6, 768, dtype=F32),
            shape(8, 128, dtype=F32),
            shape(128, 768),
            shape(768, 384, dtype=F32),
            shape(384, 768, dtype=F32),
        ],
        in_specs=[pl.BlockSpec(memory_space=pltpu.HBM)] * 14,
        out_specs=[anywhere] + [vmem] * 3 + [anywhere] * 3,
        scratch_shapes=[pltpu.VMEM(dims, dtype) for dims, dtype in SCRATCH]
        + [
            pltpu.SemaphoreType.DMA((TRANSFERS,)),
            pltpu.SemaphoreType.DMA((TRANSFERS,)),
            pltpu.SemaphoreType.DMA((18,)),
        ],
        compiler_params=pltpu.CompilerParams(
            collective_id=0, has_side_effects=True, vmem_limit_bytes=60 * 1024 * 1024
        ),
    )(
        inputs,
        routes.reshape(1, 128),
        drop_mask.reshape(1, 128),
        buckets.reshape(1, 511),
        qkv_weight,
        out_weight,
        router_weight,
        attn_gain.reshape(1, 6),
        ffn_gain.reshape(1, 6),
        bias_table.reshape(1, 3),
        cotangent,
        expert_in,
        expert_out,
        jnp.asarray(choose_matrix(), BF),
    )
    grad_input, grad_qkv, grad_out, grad_small, result, grad_in, grad_eout = outputs
    final = pl.pallas_call(
        results_kernel,
        out_shape=[
            shape(128, 768),
            shape(128, 768),
            shape(6, 2304, dtype=F32),
            shape(6, 768, dtype=F32),
            shape(6, 16, dtype=F32),
            shape(1, 6, dtype=F32),
            shape(1, 6, dtype=F32),
            shape(1, 3, dtype=F32),
            shape(768, 384, dtype=F32),
            shape(384, 768, dtype=F32),
        ],
        in_specs=[vmem] * 7,
        out_specs=[anywhere] * 4 + [vmem] * 4 + [anywhere] * 2,
        scratch_shapes=[pltpu.SemaphoreType.DMA((6,))],
        compiler_params=pltpu.CompilerParams(vmem_limit_bytes=60 * 1024 * 1024),
    )(result, grad_input, grad_qkv, grad_out, grad_small, grad_in, grad_eout)
    return (
        *final[:5],
        final[5].reshape(6),
        final[6].reshape(6),
        final[7].reshape(3),
        *final[8:],
    )


def solution(mesh):
    placed = (
        P(("fsdp", "sp"), None),
        P(("fsdp", "sp"), None),
        P(("fsdp", "sp"), None),
        P(("fsdp", "sp")),
        P(),
        P(("fsdp", "sp"), None),
        P(("fsdp", "sp"), None),
        P(("fsdp", "sp"), None),
        P(("fsdp", "sp")),
        P(("fsdp", "sp")),
        P(("fsdp", "sp")),
        P(None, ("fsdp", "sp")),
        P(("fsdp", "sp"), None),
    )
    return jax.shard_map(
        body,
        mesh=mesh,
        in_specs=placed,
        out_specs=(
            P(("fsdp", "sp"), None),
            P(("fsdp", "sp"), None),
            P(("fsdp", "sp"), None),
            P(("fsdp", "sp"), None),
            P(("fsdp", "sp"), None),
            P(("fsdp", "sp")),
            P(("fsdp", "sp")),
            P(("fsdp", "sp")),
            P(None, ("fsdp", "sp")),
            P(("fsdp", "sp"), None),
        ),
        check_vma=False,
    )
```
